256 devices in a mesh: dp: 32 (over x, y, z_lo), ctx: 8 (over z_hi, core).
Axes of the slice: x: 4, y: 4, z: 8 (z_hi: 4, z_lo: 2; z = z_hi * 2 + z_lo), core: 2. Of those that a mesh axis runs over, the one named last changes fastest.
Arguments:
- queries: bfloat16 [32, 1024, 4096], P('dp', 'ctx'), may hold values from -80 to 80
- keys: bfloat16 [32, 1024, 512], P('dp', 'ctx'), may hold values from -80 to 80
- values: bfloat16 [32, 1024, 512], P('dp', 'ctx'), may hold values from -6 to 6
- q_gain: float32 [128], replicated, may hold values from 0.8 to 2
- k_gain: float32 [128], replicated, may hold values from 0.8 to 2
- out_grad: bfloat16 [32, 1024, 4096], P('dp', 'ctx'), may hold values from -18 to 18
- block_order: int32 [32, 8], P('dp'), may hold values from 0 to 7, each once within a row
Outputs:
- grad_queries: bfloat16 [32, 1024, 4096], P('dp', 'ctx')
- grad_keys: bfloat16 [32, 1024, 512], P('dp', 'ctx')
- grad_values: bfloat16 [32, 1024, 512], P('dp', 'ctx')
- grad_q_gain: float32 [128], replicated
- grad_k_gain: float32 [128], replicated
The draws below stay inside these ranges and needn't reach their ends.
Inputs may be any that keep to these rules, and one draw needn't show every extreme that they name: `block_order`: each row lists every block index once.
All inputs are finite; a program needn't handle non-finite values.
Results may differ from the reference program's by a relative error of at most 0.03.
Values may be sent and summed in bfloat16 or wider, within the bound.
A program may use at most 128 MiB of HBM per device.

```python
import math
from functools import partial
import jax
import jax.numpy as jnp
from jax import lax

HQ = 32
HK = 4
HD = 128
GROUP = 8
TOK_DEV = 128
SEQS = 32
LEN = 1024
N_CTX = 8


def shaped_field(key, width):
    first = jax.random.fold_in(key, 0)
    third = jax.random.fold_in(key, 2)
    fourth = jax.random.fold_in(key, 3)
    normal_part = jax.random.normal(first, (SEQS, LEN, width), jnp.float32)
    base = normal_part
    base = jnp.clip(base, -4.0, 4.0)
    columns = jnp.exp(jax.random.uniform(third, (width,), jnp.float32, 0.0, math.log(10.0)))
    row_scale = jnp.exp(jax.random.uniform(fourth, (SEQS, LEN, 1), jnp.float32, math.log(0.5), math.log(2.0)))
    return base * columns * row_scale


def draw_queries(key, part):
    key = jax.random.fold_in(key, 11)
    return shaped_field(key, HQ * HD).astype(jnp.bfloat16)


def draw_keys(key, part):
    key = jax.random.fold_in(key, 12)
    return shaped_field(key, HK * HD).astype(jnp.bfloat16)


def ramped_field(key):
    first = jax.random.fold_in(key, 0)
    normal_part = jax.random.normal(first, (SEQS, LEN, HQ * HD), jnp.float32)
    base = jnp.clip(normal_part, -4.0, 4.0)
    seq_ramp = jnp.arange(SEQS, dtype=jnp.float32) / max(SEQS - 1, 1)
    row_ramp = jnp.arange(LEN, dtype=jnp.float32) / max(LEN - 1, 1)
    ramp = 0.5 * jnp.power(3.0, seq_ramp)[:, None, None] * jnp.power(3.0, row_ramp)[None, :, None]
    return base * ramp


def draw_out_grad(key, part):
    key = jax.random.fold_in(key, 13)
    return ramped_field(key).astype(jnp.bfloat16)


def block_levels(stream_key, dims, shards, least, high):
    factor_of, own = 1.0, jax.random.fold_in(stream_key, 6)
    for axis_at, shards_of in shards:
        draws = jnp.exp(jax.random.uniform(jax.random.fold_in(own, axis_at), (shards_of,), jnp.float32, least / len(shards), high / len(shards)))
        factor_of = factor_of * jnp.repeat(draws, dims[axis_at] // shards_of).reshape([-1 if axis == axis_at else 1 for axis in range(len(dims))])
    return factor_of


def bell_draw(rng, extent, scale, most, shards=(), kind=jnp.bfloat16):
    values = jax.random.normal(rng, extent, jnp.float32) * scale
    if len(shards) > 0:
        values = block_levels(rng, extent, shards, -0.22, 0.18) * values
    return jnp.clip(values, min=-most, max=most).astype(kind)


def setup_inputs(seed: int = 0) -> dict:
    key_list = jax.random.split(jax.random.key(seed), 8)
    queries = draw_queries(jax.random.fold_in(key_list[7], 71), 0)
    keys = draw_keys(jax.random.fold_in(key_list[7], 71), 0)
    values = bell_draw(key_list[2], (SEQS, LEN, HK * HD), 1.0, 6.0, ((0, 32), (1, 8)))
    q_gain = jnp.clip(jnp.exp(jax.random.uniform(key_list[3], (HD,), jnp.float32, math.log(0.8), math.log(2.0))), 0.8, 2.0)
    k_gain = jnp.clip(jnp.exp(jax.random.uniform(key_list[4], (HD,), jnp.float32, math.log(0.8), math.log(2.0))), 0.8, 2.0)
    out_grad = draw_out_grad(jax.random.fold_in(key_list[7], 71), 0)
    block_order = jax.vmap(lambda own: jax.random.permutation(own, N_CTX))(jax.random.split(key_list[6], SEQS)).reshape((SEQS, N_CTX)).astype(jnp.int32)
    return {"queries": queries, "keys": keys, "values": values, "q_gain": q_gain, "k_gain": k_gain, "out_grad": out_grad, "block_order": block_order}


EPS = 1e-06

def to_low(values_in):
    return lax.optimization_barrier(values_in.astype(jnp.bfloat16)).astype(jnp.float32)

def unit_norm(row_block, heads):
    blocks = row_block.astype(jnp.float32).reshape(row_block.shape[0], heads, HD)
    factor = lax.rsqrt(lax.optimization_barrier(jnp.mean(blocks * blocks, -1, keepdims=True)) + EPS)
    return (blocks * factor, factor)

def norm_back(gradient, unit_rows, factor, gain_vec):
    scaled = gradient * gain_vec
    return factor * (scaled - unit_rows * lax.optimization_barrier(jnp.mean(scaled * unit_rows, -1, keepdims=True)))

def one_sequence(q_gain, k_gain, items):
    queries, keys, values, out_grad, block_ids = items
    row_ids = jnp.arange(LEN, dtype=jnp.int32)
    positions = block_ids[row_ids // TOK_DEV] * TOK_DEV + row_ids % TOK_DEV
    scale = 1.0 / math.sqrt(HD)
    q_unit, q_factor = unit_norm(queries, HQ)
    k_unit, k_factor = unit_norm(keys, HK)
    q_normed = to_low(q_unit * q_gain).reshape(LEN, HK, GROUP, HD)
    k_normed = to_low(k_unit * k_gain)
    value_heads = values.astype(jnp.float32).reshape(LEN, HK, HD)
    grad_heads = out_grad.astype(jnp.float32).reshape(LEN, HK, GROUP, HD)
    visible = positions[None, :] <= positions[:, None]
    scores = jnp.einsum('ikgd,jkd->kgij', q_normed, k_normed) * scale
    weights = jnp.where(visible, jnp.exp(scores), 0.0)
    totals = lax.optimization_barrier(jnp.sum(weights, -1))
    attended = jnp.einsum('kgij,jkd->ikgd', to_low(weights), value_heads)
    attended = (attended / jnp.transpose(totals, (2, 0, 1))[..., None]).astype(jnp.bfloat16)
    log_totals = jnp.log(totals)
    row_dots = jnp.transpose(lax.optimization_barrier(jnp.sum(grad_heads * attended.astype(jnp.float32), -1)), (1, 2, 0))
    probs = jnp.where(visible, jnp.exp(scores - log_totals[..., None]), 0.0)
    grad_values = jnp.einsum('kgij,ikgd->jkd', to_low(probs), grad_heads)
    dprobs = jnp.einsum('ikgd,jkd->kgij', grad_heads, value_heads)
    dscores = to_low(probs * (dprobs - row_dots[..., None]))
    grad_qn = jnp.einsum('kgij,jkd->ikgd', dscores, k_normed) * scale
    grad_kn = jnp.einsum('kgij,ikgd->jkd', dscores, q_normed) * scale
    grad_qn = grad_qn.reshape(LEN, HQ, HD)
    q_gain_part = lax.optimization_barrier(jnp.sum(grad_qn * q_unit, axis=(0, 1)))
    k_gain_part = lax.optimization_barrier(jnp.sum(grad_kn * k_unit, axis=(0, 1)))
    grad_queries = norm_back(grad_qn, q_unit, q_factor, q_gain).astype(jnp.bfloat16).reshape(LEN, HQ * HD)
    grad_keys = norm_back(grad_kn, k_unit, k_factor, k_gain).astype(jnp.bfloat16).reshape(LEN, HK * HD)
    return (grad_queries, grad_keys, grad_values.astype(jnp.bfloat16).reshape(LEN, HK * HD), q_gain_part, k_gain_part)

def reference(queries, keys, values, q_gain, k_gain, out_grad, block_order):
    results = lax.map(partial(one_sequence, q_gain, k_gain), (queries, keys, values, out_grad, block_order))
    return (results[0], results[1], results[2], lax.optimization_barrier(jnp.sum(results[3], 0)), lax.optimization_barrier(jnp.sum(results[4], 0)))
```

```python
import math

import jax
import jax.numpy as jnp
from jax import lax
from jax.experimental import pallas as pl
from jax.experimental.pallas import tpu as pltpu
from jax.sharding import PartitionSpec as P

HQ = 32
HK = 4
HD = 128
T = 128
EPS = 1e-06
SCALE = 1.0 / math.sqrt(HD)
EXP2_SCALE = SCALE * math.log2(math.e)
NEG = -1e30
BF = jnp.bfloat16
F32 = jnp.float32
MESH = pl.DeviceIdType.MESH
NT = (((1,), (1,)), ((), ()))
NN = (((1,), (0,)), ((), ()))

STEP_FORWARD = 3
STEP_REDUCE = 11
STEP_FINISH = 15


def dot(a, b, dims):
    return lax.dot_general(a, b, dims, preferred_element_type=F32)


def make_bias(bias, order, chip, core):
    keys_at = lax.broadcasted_iota(jnp.int32, (T, T), 0)
    rows_at = lax.broadcasted_iota(jnp.int32, (T, T), 1)
    for rel in range(2):
        mine = 2 * chip + (core if rel == 0 else 1 - core)
        own = order[0, mine]
        for j in range(8):
            key_pos = order[0, j] * T + keys_at
            row_pos = own * T + rows_at
            bias[rel, j] = jnp.where(key_pos <= row_pos, 0.0, NEG)


def chunk(u, rel, hp, q_buf, g_buf, kv, kt, bias, q_gain, acc, dq_buf, gain_acc, e_scr, d_scr, p_scr, ds_scr):
    cols = pl.ds(pl.multiple_of(hp * 256, 256), 256)
    q2 = q_buf[u, rel, :, cols]
    g2 = g_buf[u, rel, :, cols]
    q = jnp.concatenate([q2[:, :HD], q2[:, HD:]], 0).astype(F32)
    g = jnp.concatenate([g2[:, :HD], g2[:, HD:]], 0)
    factor = lax.rsqrt(jnp.mean(q * q, -1, keepdims=True) + EPS)
    q_unit = q * factor
    gain = q_gain[...]
    qn = (q_unit * gain).astype(BF)
    e_scr[...] = dot(kv[u, 0].reshape(8 * T, HD), qn, NT)
    d_scr[...] = dot(kv[u, 1].reshape(8 * T, HD), g, NT)
    total = jnp.zeros((8, 256), F32)
    cross = jnp.zeros((8, 256), F32)
    half = 64
    for b in range(8 * T // half):
        at = pl.ds(b * half, half)
        j, off = divmod(b * half, T)
        tile = bias[rel, j, off : off + half, :]
        tile = jnp.concatenate([tile, tile], 1)
        e = jnp.exp2(e_scr[at, :] * EXP2_SCALE + tile)
        e_scr[at, :] = e
        total = total + jnp.sum(e.reshape(half // 8, 8, 256), 0)
        cross = cross + jnp.sum((e * d_scr[at, :]).reshape(half // 8, 8, 256), 0)
    inv = 1.0 / jnp.sum(total, 0, keepdims=True)
    row_dots = jnp.sum(cross, 0, keepdims=True) * inv
    for b in range(8 * T // half):
        at = pl.ds(b * half, half)
        p = e_scr[at, :] * inv
        p_scr[at, :] = p.astype(BF)
        ds_scr[at, :] = (p * (d_scr[at, :] - row_dots)).astype(BF)
    acc[u, 1] += dot(p_scr[...], g, NN)
    acc[u, 0] += dot(ds_scr[...], qn, NN)
    dq = dot(kt[...], ds_scr[...], NN).T * SCALE
    gain_acc[0] += jnp.sum((dq * q_unit).reshape(32, 8, HD), 0)
    scaled = dq * gain
    mean = jnp.mean(scaled * q_unit, -1, keepdims=True)
    out = (factor * (scaled - q_unit * mean)).astype(BF)
    dq_buf[u, rel, :, cols] = jnp.concatenate([out[:T], out[T:]], 1)


def kernel(
    order,
    q_hbm,
    k_hbm,
    v_hbm,
    q_gain,
    k_gain,
    g_hbm,
    dq_hbm,
    dk_hbm,
    dv_hbm,
    q_gain_out,
    k_gain_out,
    k_in,
    v_in,
    q_buf,
    g_buf,
    own_kv,
    kv,
    kt,
    bias,
    acc,
    dq_buf,
    gain_acc,
    e_scr,
    d_scr,
    p_scr,
    ds_scr,
    b1_out,
    b1_in,
    b2_out,
    b2_in,
    sib_out,
    sib_in,
    dk_buf,
    dv_buf,
    g1_in,
    g2_in,
    g3_in,
    load_sem,
    qx_send,
    qx_recv,
    s1_send,
    s1_recv,
    s2_send,
    s2_recv,
    sk_send,
    sk_recv,
    b1_send,
    b1_recv,
    b2_send,
    b2_recv,
    sb_send,
    sb_recv,
    out_sem,
    ox_send,
    ox_recv,
    g1_send,
    g1_recv,
    g2_send,
    g2_recv,
    g3_send,
    g3_recv,
    fin_sem,
):
    ctx = lax.axis_index("ctx")
    dp = lax.axis_index("dp")
    chip = ctx // 2
    core = ctx % 2
    other = 1 - core
    sibling = 2 * chip + other
    nxt = lax.rem(chip + 1, 4)
    prv = lax.rem(chip + 3, 4)
    opp = lax.rem(chip + 2, 4)
    near = (nxt, prv)
    dp_x = dp // 8
    dp_y = (dp // 2) % 4
    dp_z = dp % 2
    xz = dp_x * 2 + dp_z

    def xz_peer(m):
        return (m // 2) * 8 + dp_y * 2 + m % 2

    def y_peer(m):
        return dp_x * 8 + m * 2 + dp_z

    def remote(src, dst, ssem, rsem, dev):
        return pltpu.make_async_remote_copy(
            src_ref=src, dst_ref=dst, send_sem=ssem, recv_sem=rsem, device_id=dev, device_id_type=MESH
        )

    def head_cols(core_at, u):
        return pl.ds(pl.multiple_of(core_at * 2048 + u * 1024, 1024), 1024)

    load_k = pltpu.make_async_copy(k_hbm.at[0], k_in, load_sem.at[0])
    load_v = pltpu.make_async_copy(v_hbm.at[0], v_in, load_sem.at[1])
    load_k.start()
    load_v.start()
    load_q = []
    for u in range(2):
        pair = (
            pltpu.make_async_copy(q_hbm.at[0, :, head_cols(core, u)], q_buf.at[u, 0], load_sem.at[2 + 2 * u]),
            pltpu.make_async_copy(g_hbm.at[0, :, head_cols(core, u)], g_buf.at[u, 0], load_sem.at[3 + 2 * u]),
        )
        load_q.append(pair)
        for c in pair:
            c.start()

    barrier = pltpu.get_barrier_semaphore()
    for r in range(1, 8):
        pl.semaphore_signal(barrier, inc=1, device_id={"ctx": lax.rem(ctx + r, 8)}, device_id_type=MESH)
        pl.semaphore_signal(barrier, inc=1, device_id={"dp": xz_peer(lax.rem(xz + r, 8))}, device_id_type=MESH)
    for r in range(1, 4):
        pl.semaphore_signal(barrier, inc=1, device_id={"dp": y_peer(lax.rem(dp_y + r, 4))}, device_id_type=MESH)

    load_k.wait()
    load_v.wait()
    k_gain_row = k_gain[...]
    for h in range(HK):
        block = k_in[:, h * HD : (h + 1) * HD].astype(F32)
        factor = lax.rsqrt(jnp.mean(block * block, -1, keepdims=True) + EPS)
        own_kv[h, 0] = (block * factor * k_gain_row).astype(BF)
        own_kv[h, 1] = v_in[:, h * HD : (h + 1) * HD]
    for u in range(2):
        for part in range(2):
            kv[u, part, ctx] = own_kv[2 * core + u, part]
    gain_acc[...] = jnp.zeros_like(gain_acc)
    acc[...] = jnp.zeros_like(acc)

    pl.semaphore_wait(barrier, 17)

    def stage1(u, d, dest_core, part):
        return remote(
            own_kv.at[2 * dest_core + u, part],
            kv.at[u, part, ctx],
            s1_send.at[u, d, dest_core, part],
            s1_recv.at[u, d, core, part],
            {"ctx": 2 * near[d] + dest_core},
        )

    def stage1_arrival(u, d, src_core, part):
        j = 2 * near[1 - d] + src_core
        return remote(
            kv.at[u, part, j], kv.at[u, part, j], s1_send.at[u, d, src_core, part], s1_recv.at[u, d, src_core, part], {"ctx": sibling}
        )

    def sibling_kv(u):
        return remote(own_kv.at[2 * other + u], kv.at[u, :, ctx], sk_send.at[u], sk_recv.at[u], {"ctx": sibling})

    def sibling_kv_arrival(u):
        return remote(own_kv.at[2 * core + u], kv.at[u, :, sibling], sk_send.at[u], sk_recv.at[u], {"ctx": sibling})

    def stage2(u, d, src_core):
        j = 2 * near[1 - d] + src_core
        return remote(
            kv.at[u, d, j], kv.at[u, d, j], s2_send.at[u, d, src_core], s2_recv.at[u, d, src_core], {"ctx": 2 * near[d] + core}
        )

    def stage2_arrival(u, d, src_core):
        j = 2 * opp + src_core
        return remote(
            kv.at[u, d, j], kv.at[u, d, j], s2_send.at[u, d, src_core], s2_recv.at[u, d, src_core], {"ctx": sibling}
        )

    def q_exchange(u):
        return (
            remote(q_hbm.at[0, :, head_cols(other, u)], q_buf.at[u, 1], qx_send.at[u, 0], qx_recv.at[u, 0], {"ctx": sibling}),
            remote(g_hbm.at[0, :, head_cols(other, u)], g_buf.at[u, 1], qx_send.at[u, 1], qx_recv.at[u, 1], {"ctx": sibling}),
        )

    for u in range(2):
        for first in range(2):
            for d in range(2):
                for dest_core in range(2):
                    stage1(u, d, dest_core, d if first == 0 else 1 - d).start()
        sibling_kv(u).start()
        for c in q_exchange(u):
            c.start()

    make_bias(bias, order, chip, core)

    def forward(u):
        for src_core in range(2):
            for d in range(2):
                stage1_arrival(u, d, src_core, d).wait_recv()
                stage2(u, d, src_core).start()

    def finish_gather(u):
        for src_core in range(2):
            for d in range(2):
                stage1_arrival(u, d, src_core, 1 - d).wait_recv()
        sibling_kv_arrival(u).wait_recv()
        for src_core in range(2):
            for d in range(2):
                stage2_arrival(u, d, src_core).wait_recv()
        kt[...] = kv[u, 0].reshape(8 * T, HD).T

    def b1(u, d):
        return remote(b1_out.at[u, d], b1_in.at[u, d], b1_send.at[u, d], b1_recv.at[u, d], {"ctx": 2 * near[d] + core})

    def b2(u, d, dest_core, part):
        return remote(
            b2_out.at[u, d, dest_core, part],
            b2_in.at[u, d, core, part],
            b2_send.at[u, d, dest_core, part],
            b2_recv.at[u, d, core, part],
            {"ctx": 2 * near[d] + dest_core},
        )

    def b2_arrival(u, d, src_core, part):
        return remote(
            b2_out.at[u, d, src_core, part],
            b2_in.at[u, d, src_core, part],
            b2_send.at[u, d, src_core, part],
            b2_recv.at[u, d, src_core, part],
            {"ctx": sibling},
        )

    def sibling_sum(u):
        return remote(sib_out.at[u], sib_in.at[u], sb_send.at[u], sb_recv.at[u], {"ctx": sibling})

    def partial_sum(u, part, j):
        block = acc[u, part, pl.ds(pl.multiple_of(j * T, T), T), :]
        return block * SCALE if part == 0 else block

    def reduce_start(u):
        for d in range(2):
            for dest_core in range(2):
                b1_out[u, d, dest_core] = partial_sum(u, d, 2 * opp + dest_core).astype(BF)
            b1(u, d).start()
        for d in range(2):
            for dest_core in range(2):
                b2_out[u, d, dest_core, 1 - d] = partial_sum(u, 1 - d, 2 * near[d] + dest_core).astype(BF)
                b2(u, d, dest_core, 1 - d).start()
        for part in range(2):
            sib_out[u, part] = partial_sum(u, part, sibling).astype(BF)
        sibling_sum(u).start()
        k_rows = kv[u, 0].reshape(8 * T, HD).astype(F32)
        gain_acc[1] += jnp.sum((acc[u, 0] * k_rows).reshape(T, 8, HD), 0)

    def reduce_middle(u):
        for d in range(2):
            b1(u, d).wait_recv()
            for dest_core in range(2):
                own = partial_sum(u, d, 2 * near[d] + dest_core)
                b2_out[u, d, dest_core, d] = (own + b1_in[u, d, dest_core].astype(F32)).astype(BF)
                b2(u, d, dest_core, d).start()

    def reduce_finish(u):
        sibling_sum(u).wait_recv()
        for d in range(2):
            for src_core in range(2):
                for part in range(2):
                    b2_arrival(u, d, src_core, part).wait_recv()
        for rel in range(2):
            at = core if rel == 0 else other
            sums = []
            for part in range(2):
                own = partial_sum(u, part, ctx) if rel == 0 else sib_in[u, part].astype(F32)
                sums.append(own + b2_in[u, 0, at, part].astype(F32) + b2_in[u, 1, at, part].astype(F32))
            cols = pl.ds(pl.multiple_of(at * 256 + u * HD, HD), HD)
            block = k_in[:, cols].astype(F32)
            factor = lax.rsqrt(jnp.mean(block * block, -1, keepdims=True) + EPS)
            unit = block * factor
            scaled = sums[0] * k_gain_row
            mean = jnp.mean(scaled * unit, -1, keepdims=True)
            dk_buf[:, cols] = (factor * (scaled - unit * mean)).astype(BF)
            dv_buf[:, cols] = sums[1].astype(BF)

    def out_local(u):
        return pltpu.make_async_copy(dq_buf.at[u, 0], dq_hbm.at[0, :, head_cols(core, u)], out_sem.at[u])

    def out_remote(u):
        return remote(dq_buf.at[u, 1], dq_hbm.at[0, :, head_cols(core, u)], ox_send.at[u], ox_recv.at[u], {"ctx": sibling})

    def out_arrival(u):
        return remote(dq_buf.at[u, 1], dq_hbm.at[0, :, head_cols(other, u)], ox_send.at[u], ox_recv.at[u], {"ctx": sibling})

    forward(0)
    finish_gather(0)

    def step(t, carry):
        u = t // 8
        rel = (t % 8) // 4
        hp = t % 4

        @pl.when(t == 0)
        def _():
            for c in load_q[0]:
                c.wait()

        @pl.when(t == STEP_FORWARD)
        def _():
            forward(1)

        @pl.when(t == 4)
        def _():
            out_local(0).start()
            for c in q_exchange(0):
                c.wait_recv()

        @pl.when(t == 8)
        def _():
            out_remote(0).start()
            reduce_start(0)
            finish_gather(1)
            for c in load_q[1]:
                c.wait()

        @pl.when(t == STEP_REDUCE)
        def _():
            reduce_middle(0)

        @pl.when(t == 12)
        def _():
            out_local(1).start()
            for c in q_exchange(1):
                c.wait_recv()

        @pl.when(t == STEP_FINISH)
        def _():
            reduce_finish(0)

        chunk(u, rel, hp, q_buf, g_buf, kv, kt, bias, q_gain, acc, dq_buf, gain_acc, e_scr, d_scr, p_scr, ds_scr)
        return carry

    lax.fori_loop(0, 16, step, 0)
    reduce_start(1)
    out_remote(1).start()

    def g1(r):
        return remote(g1_in.at[ctx], g1_in.at[ctx], g1_send.at[r], g1_recv.at[ctx], {"ctx": lax.rem(ctx + r, 8)})

    def g1_arrival(r):
        j = lax.rem(ctx + r, 8)
        return remote(g1_in.at[j], g1_in.at[j], g1_send.at[r], g1_recv.at[j], {"ctx": sibling})

    def g2(r):
        return remote(g2_in.at[xz], g2_in.at[xz], g2_send.at[r], g2_recv.at[xz], {"dp": xz_peer(lax.rem(xz + r, 8))})

    def g2_arrival(r):
        j = lax.rem(xz + r, 8)
        return remote(g2_in.at[j], g2_in.at[j], g2_send.at[r], g2_recv.at[j], {"ctx": sibling})

    def g3(r):
        return remote(g3_in.at[dp_y], g3_in.at[dp_y], g3_send.at[r], g3_recv.at[dp_y], {"dp": y_peer(lax.rem(dp_y + r, 4))})

    def g3_arrival(r):
        j = lax.rem(dp_y + r, 4)
        return remote(g3_in.at[j], g3_in.at[j], g3_send.at[r], g3_recv.at[j], {"ctx": sibling})

    g1_in[ctx] = gain_acc[...]
    for r in range(1, 8):
        g1(r).start()
    reduce_middle(1)
    for r in range(1, 8):
        g1_arrival(r).wait_recv()
    g2_in[xz] = jnp.sum(g1_in[...], 0)
    for r in range(1, 8):
        g2(r).start()
    for r in range(1, 8):
        g2_arrival(r).wait_recv()
    g3_in[dp_y] = jnp.sum(g2_in[...], 0)
    for r in range(1, 4):
        g3(r).start()
    reduce_finish(1)
    fin_k = pltpu.make_async_copy(dk_buf, dk_hbm.at[0], fin_sem.at[0])
    fin_v = pltpu.make_async_copy(dv_buf, dv_hbm.at[0], fin_sem.at[1])
    fin_k.start()
    fin_v.start()
    for r in range(1, 4):
        g3_arrival(r).wait_recv()
    gains = jnp.sum(jnp.sum(g3_in[...], 0), 1, keepdims=True)
    q_gain_out[...] = gains[0]
    k_gain_out[...] = gains[1] * SCALE / k_gain_row

    for u in range(2):
        for d in range(2):
            for dest_core in range(2):
                for part in range(2):
                    stage1(u, d, dest_core, part).wait_send()
                    b2(u, d, dest_core, part).wait_send()
                stage2(u, d, dest_core).wait_send()
            b1(u, d).wait_send()
        sibling_kv(u).wait_send()
        sibling_sum(u).wait_send()
        for c in q_exchange(u):
            c.wait_send()
        out_local(u).wait()
        out_remote(u).wait_send()
        out_arrival(u).wait_recv()
    for r in range(1, 8):
        g1(r).wait_send()
        g2(r).wait_send()
    for r in range(1, 4):
        g3(r).wait_send()
    fin_k.wait()
    fin_v.wait()


def on_device(queries, keys, values, q_gain, k_gain, out_grad, block_order):
    hbm = pl.BlockSpec(memory_space=pl.ANY)
    vmem = pl.BlockSpec(memory_space=pltpu.VMEM)
    smem = pl.BlockSpec(memory_space=pltpu.SMEM)
    dma = pltpu.SemaphoreType.DMA
    dq, dk, dv, dqg, dkg = pl.pallas_call(
        kernel,
        out_shape=(
            jax.ShapeDtypeStruct(queries.shape, BF),
            jax.ShapeDtypeStruct(keys.shape, BF),
            jax.ShapeDtypeStruct(values.shape, BF),
            jax.ShapeDtypeStruct((1, HD), F32),
            jax.ShapeDtypeStruct((1, HD), F32),
        ),
        in_specs=[smem, hbm, hbm, hbm, vmem, vmem, hbm],
        out_specs=(hbm, hbm, hbm, vmem, vmem),
        scratch_shapes=[
            pltpu.VMEM((T, HK * HD), BF),
            pltpu.VMEM((T, HK * HD), BF),
            pltpu.VMEM((2, 2, T, 1024), BF),
            pltpu.VMEM((2, 2, T, 1024), BF),
            pltpu.VMEM((HK, 2, T, HD), BF),
            pltpu.VMEM((2, 2, 8, T, HD), BF),
            pltpu.VMEM((HD, 8 * T), BF),
            pltpu.VMEM((2, 8, T, T), F32),
            pltpu.VMEM((2, 2, 8 * T, HD), F32),
            pltpu.VMEM((2, 2, T, 1024), BF),
            pltpu.VMEM((2, 8, HD), F32),
            pltpu.VMEM((8 * T, 256), F32),
            pltpu.VMEM((8 * T, 256), F32),
            pltpu.VMEM((8 * T, 256), BF),
            pltpu.VMEM((8 * T, 256), BF),
            pltpu.VMEM((2, 2, 2, T, HD), BF),
            pltpu.VMEM((2, 2, 2, T, HD), BF),
            pltpu.VMEM((2, 2, 2, 2, T, HD), BF),
            pltpu.VMEM((2, 2, 2, 2, T, HD), BF),
            pltpu.VMEM((2, 2, T, HD), BF),
            pltpu.VMEM((2, 2, T, HD), BF),
            pltpu.VMEM((T, HK * HD), BF),
            pltpu.VMEM((T, HK * HD), BF),
            pltpu.VMEM((8, 2, 8, HD), F32),
            pltpu.VMEM((8, 2, 8, HD), F32),
            pltpu.VMEM((4, 2, 8, HD), F32),
            dma((6,)),
            dma((2, 2)),
            dma((2, 2)),
            dma((2, 2, 2, 2)),
            dma((2, 2, 2, 2)),
            dma((2, 2, 2)),
            dma((2, 2, 2)),
            dma((2,)),
            dma((2,)),
            dma((2, 2)),
            dma((2, 2)),
            dma((2, 2, 2, 2)),
            dma((2, 2, 2, 2)),
            dma((2,)),
            dma((2,)),
            dma((2,)),
            dma((2,)),
            dma((2,)),
            dma((8,)),
            dma((8,)),
            dma((8,)),
            dma((8,)),
            dma((4,)),
            dma((4,)),
            dma((2,)),
        ],
        compiler_params=pltpu.CompilerParams(
            collective_id=0, has_side_effects=True, vmem_limit_bytes=40 * 1024 * 1024
        ),
    )(block_order, queries, keys, values, q_gain.reshape(1, HD), k_gain.reshape(1, HD), out_grad)
    return dq, dk, dv, dqg.reshape(HD), dkg.reshape(HD)


def solution(mesh):
    placed = (
        P("dp", "ctx", None),
        P("dp", "ctx", None),
        P("dp", "ctx", None),
        P(),
        P(),
        P("dp", "ctx", None),
        P("dp", None),
    )
    return jax.shard_map(
        on_device,
        mesh=mesh,
        in_specs=placed,
        out_specs=(P("dp", "ctx", None), P("dp", "ctx", None), P("dp", "ctx", None), P(), P()),
        check_vma=False,
    )
```

```python
import math

import jax
import jax.numpy as jnp
from jax import lax
from jax.experimental import pallas as pl
from jax.experimental.pallas import tpu as pltpu
from jax.sharding import PartitionSpec as P

HK = 4
HD = 128
T = 128
KEYS = 8 * T
ROWS = 16 * T
EPS = 1e-06
SCALE = 1.0 / math.sqrt(HD)
EXP2_SCALE = SCALE * math.log2(math.e)
NEG = -1e30
BF = jnp.bfloat16
F32 = jnp.float32
MESH = pl.DeviceIdType.MESH
NT = (((1,), (1,)), ((), ()))
NN = (((1,), (0,)), ((), ()))

STEP_FORWARD = 6
STEP_REDUCE = 6
EARLY = 4


def dot(a, b, dims):
    return lax.dot_general(a, b, dims, preferred_element_type=F32)


def make_bias(bias, order, chip, core):
    keys_at = lax.broadcasted_iota(jnp.int32, (T, T), 0)
    rows_at = lax.broadcasted_iota(jnp.int32, (T, T), 1)
    for rel in range(2):
        own = order[0, 2 * chip + (core if rel == 0 else 1 - core)]
        for j in range(8):
            block = order[0, 2 * lax.rem(chip + j // 2, 4) + j % 2]
            bias[rel, j] = jnp.where(block * T + keys_at <= own * T + rows_at, 0.0, NEG)


def prepare(u, rel, hp, q_buf, g_buf, q_normed, g_cols, q_unit, q_factor, gain_cols):
    cols = pl.ds(pl.multiple_of(hp * 256, 256), 256)
    out = pl.ds(pl.multiple_of(rel * 1024 + hp * 256, 256), 256)
    q2 = q_buf[u, rel, :, cols].astype(F32)
    g2 = g_buf[u, rel, :, cols].astype(F32)
    q = jnp.concatenate([q2[:, :HD].T, q2[:, HD:].T], 1)
    factor = lax.rsqrt(jnp.mean(q * q, 0, keepdims=True) + EPS)
    unit = q * factor
    q_factor[u, :, out] = jnp.broadcast_to(factor, (8, 256))
    q_unit[u, :, out] = unit
    q_normed[u, :, out] = (unit * gain_cols[...]).astype(BF)
    g_cols[u, :, out] = jnp.concatenate([g2[:, :HD].T, g2[:, HD:].T], 1).astype(BF)


def softmax_part(u, r, kv, q_normed, g_cols, bias, e_all, x_all, stat, w_all):
    rel = r // 4
    cols = pl.ds(pl.multiple_of(r * 256, 256), 256)
    qn = q_normed[u, :, cols]
    g = g_cols[u, :, cols]
    total = jnp.zeros((8, 256), F32)
    cross = jnp.zeros((8, 256), F32)
    half = T // 2
    for j in range(0, 8, 2):
        s = dot(kv[u, 0, j : j + 2].reshape(2 * T, HD), qn, NN)
        d = dot(kv[u, 1, j : j + 2].reshape(2 * T, HD), g, NN)
        for b in range(4):
            at, row = b * half, j * T + b * half
            tile = bias[rel, j + b // 2, (b % 2) * half : (b % 2 + 1) * half, :]
            tile = jnp.concatenate([tile, tile], 1)
            e = jnp.exp2(s[at : at + half] * EXP2_SCALE + tile)
            x = e * d[at : at + half]
            total = total + jnp.sum(e.reshape(half // 8, 8, 256), 0)
            cross = cross + jnp.sum(x.reshape(half // 8, 8, 256), 0)
            e_all[u, row : row + half, cols] = e.astype(BF)
            x_all[u, row : row + half, cols] = x.astype(BF)
    inv = 1.0 / jnp.sum(total, 0, keepdims=True)
    row_dots = jnp.sum(cross, 0, keepdims=True) * inv
    stat[u, 0, :, cols] = jnp.broadcast_to(inv * SCALE, (8, 256))
    stat[u, 1, :, cols] = jnp.broadcast_to(row_dots, (8, 256))
    scaled = qn.astype(F32) * inv
    w_all[u, 0:128, cols] = (g.astype(F32) * inv).astype(BF)
    w_all[u, 128:256, cols] = (scaled * -row_dots).astype(BF)
    w_all[u, 256:384, cols] = scaled.astype(BF)


def key_part(u, slot, e_all, x_all, w_all):
    at = slice(slot * 256, slot * 256 + 256)
    both = dot(e_all[u, at, :], w_all[u, 0:256, :], NT)
    dk = (both[:, HD:] + dot(x_all[u, at, :], w_all[u, 256:384, :], NT)) * SCALE
    return dk, both[:, :HD]


def query_part(u, r, kt, e_all, x_all, stat, q_unit, q_factor, gain_cols, dq_buf, gain_acc):
    rel = r // 2
    rows = pl.ds(pl.multiple_of(r * 512, 512), 512)
    x = dot(kt[u], x_all[u, :, rows], NN)
    e = dot(kt[u], e_all[u, :, rows], NN)
    dq = (x - e * stat[u, 1, 0:1, rows]) * stat[u, 0, 0:1, rows]
    unit = q_unit[u, :, rows]
    prod = dq * unit
    gain_acc[...] += (prod[:, :HD] + prod[:, HD:256]) + (prod[:, 256:384] + prod[:, 384:])
    gain = gain_cols[...]
    scaled = dq * jnp.concatenate([gain, gain], 1)
    mean = jnp.mean(scaled * unit, 0, keepdims=True)
    out = q_factor[u, 0:1, rows] * (scaled - unit * mean)
    cols = pl.ds(pl.multiple_of((r % 2) * 512, 512), 512)
    dq_buf[u, rel, :, cols] = jnp.concatenate([out[:, i * HD : i * HD + HD].T for i in range(4)], 1).astype(BF)


def kernel(
    order,
    q_hbm,
    k_hbm,
    v_hbm,
    q_gain,
    k_gain,
    g_hbm,
    dq_hbm,
    dk_hbm,
    dv_hbm,
    gains_out,
    k_in,
    v_in,
    q_buf,
    g_buf,
    q_normed,
    g_cols,
    q_unit,
    q_factor,
    gain_cols,
    own_kv,
    kv,
    kt,
    bias,
    e_all,
    x_all,
    stat,
    w_all,
    near_sum,
    own_sum,
    dq_buf,
    gain_acc,
    k_gain_acc,
    b1_out,
    b1_in,
    b2_out,
    b2_in,
    sib_out,
    sib_in,
    dk_buf,
    dv_buf,
    ga_in,
    gb_in,
    load_sem,
    qx_send,
    qx_recv,
    s1_send,
    s1_recv,
    s2_send,
    s2_recv,
    sk_send,
    sk_recv,
    b1_send,
    b1_recv,
    b2_send,
    b2_recv,
    sb_send,
    sb_recv,
    out_sem,
    ox_send,
    ox_recv,
    ga_send,
    ga_recv,
    gb_send,
    gb_recv,
    fin_sem,
):
    ctx = lax.axis_index("ctx")
    dp = lax.axis_index("dp")
    chip = ctx // 2
    core = ctx % 2
    other = 1 - core
    sibling = 2 * chip + other
    near = (lax.rem(chip + 1, 4), lax.rem(chip + 3, 4))
    dp_z = dp % 2
    dp_xy = dp // 2
    ring_at = dp_z * 8 + ctx

    def ring_peer(m):
        return {"dp": dp_xy * 2 + m // 8, "ctx": m % 8}

    def plane_peer(m):
        return {"dp": m * 2 + dp_z}

    def remote(src, dst, ssem, rsem, dev):
        return pltpu.make_async_remote_copy(
            src_ref=src, dst_ref=dst, send_sem=ssem, recv_sem=rsem, device_id=dev, device_id_type=MESH
        )

    def head_cols(core_at, u):
        return pl.ds(pl.multiple_of(core_at * 2048 + u * 1024, 1024), 1024)

    barrier = pltpu.get_barrier_semaphore()

    def greet(r, carry):
        pl.semaphore_signal(barrier, inc=1, device_id=ring_peer(lax.rem(ring_at + r, 16)), device_id_type=MESH)
        pl.semaphore_signal(barrier, inc=1, device_id=plane_peer(lax.rem(dp_xy + r, 16)), device_id_type=MESH)
        return carry

    load_k = pltpu.make_async_copy(k_hbm.at[0], k_in, load_sem.at[0])
    load_v = pltpu.make_async_copy(v_hbm.at[0], v_in, load_sem.at[1])
    load_k.start()
    load_v.start()
    lax.fori_loop(1, 16, greet, 0)
    load_q = []
    for u in range(2):
        pair = (
            pltpu.make_async_copy(q_hbm.at[0, :, head_cols(core, u)], q_buf.at[u, 0], load_sem.at[2 + 2 * u]),
            pltpu.make_async_copy(g_hbm.at[0, :, head_cols(core, u)], g_buf.at[u, 0], load_sem.at[3 + 2 * u]),
        )
        load_q.append(pair)
        for c in pair:
            c.start()

    load_k.wait()
    load_v.wait()
    k_gain_row = k_gain[...]
    for h in range(HK):
        block = k_in[:, h * HD : (h + 1) * HD].astype(F32)
        factor = lax.rsqrt(jnp.mean(block * block, -1, keepdims=True) + EPS)
        own_kv[h, 0] = (block * factor * k_gain_row).astype(BF)
        own_kv[h, 1] = v_in[:, h * HD : (h + 1) * HD]

    pl.semaphore_wait(barrier, 30)

    lands = (3, 1)

    def stage1(u, d, dest_core, part):
        return remote(
            own_kv.at[2 * dest_core + u, part],
            kv.at[u, part, 2 * lands[d] + core],
            s1_send.at[u, d, dest_core, part],
            s1_recv.at[u, d, core, part],
            {"ctx": 2 * near[d] + dest_core},
        )

    def stage1_arrival(u, d, src_core, part):
        at = kv.at[u, part, 2 * lands[d] + src_core]
        return remote(at, at, s1_send.at[u, d, src_core, part], s1_recv.at[u, d, src_core, part], {"ctx": sibling})

    def sibling_kv(u):
        return remote(own_kv.at[2 * other + u], kv.at[u, :, core], sk_send.at[u], sk_recv.at[u], {"ctx": sibling})

    def sibling_kv_arrival(u):
        return remote(own_kv.at[2 * core + u], kv.at[u, :, other], sk_send.at[u], sk_recv.at[u], {"ctx": sibling})

    def stage2(u, d, src_core):
        return remote(
            kv.at[u, d, 2 * lands[d] + src_core],
            kv.at[u, d, 4 + src_core],
            s2_send.at[u, d, src_core],
            s2_recv.at[u, d, src_core],
            {"ctx": 2 * near[d] + core},
        )

    def stage2_arrival(u, d, src_core):
        at = kv.at[u, d, 4 + src_core]
        return remote(at, at, s2_send.at[u, d, src_core], s2_recv.at[u, d, src_core], {"ctx": sibling})

    def q_exchange(u):
        return (
            remote(q_hbm.at[0, :, head_cols(other, u)], q_buf.at[u, 1], qx_send.at[u, 0], qx_recv.at[u, 0], {"ctx": sibling}),
            remote(g_hbm.at[0, :, head_cols(other, u)], g_buf.at[u, 1], qx_send.at[u, 1], qx_recv.at[u, 1], {"ctx": sibling}),
        )

    def gather_start(u):
        for first in range(2):
            for d in range(2):
                for dest_core in range(2):
                    stage1(u, d, dest_core, d if first == 0 else 1 - d).start()
        sibling_kv(u).start()
        for c in q_exchange(u):
            c.start()

    def forward(u):
        for src_core in range(2):
            for d in range(2):
                stage1_arrival(u, d, src_core, d).wait_recv()
                stage2(u, d, src_core).start()

    def finish_gather(u):
        for src_core in range(2):
            for d in range(2):
                stage1_arrival(u, d, src_core, 1 - d).wait_recv()
        sibling_kv_arrival(u).wait_recv()
        for src_core in range(2):
            for d in range(2):
                stage2_arrival(u, d, src_core).wait_recv()
        kt[u] = kv[u, 0].reshape(KEYS, HD).T

    def prepare_rows(u, rel):
        if rel == 0:
            for c in load_q[u]:
                c.wait()
        else:
            for c in q_exchange(u):
                c.wait_recv()

        def one(hp, carry):
            prepare(u, rel, hp, q_buf, g_buf, q_normed, g_cols, q_unit, q_factor, gain_cols)
            return carry

        lax.fori_loop(0, 4, one, 0)

    def b1(u, d):
        return remote(b1_out.at[u, d], b1_in.at[u, d], b1_send.at[u, d], b1_recv.at[u, d], {"ctx": 2 * near[d] + core})

    def b2(u, d, dest_core, part):
        return remote(
            b2_out.at[u, d, dest_core, part],
            b2_in.at[u, d, core, part],
            b2_send.at[u, d, dest_core, part],
            b2_recv.at[u, d, core, part],
            {"ctx": 2 * near[d] + dest_core},
        )

    def b2_arrival(u, d, src_core, part):
        at = b2_in.at[u, d, src_core, part]
        return remote(at, at, b2_send.at[u, d, src_core, part], b2_recv.at[u, d, src_core, part], {"ctx": sibling})

    def sibling_sum(u):
        return remote(sib_out.at[u], sib_in.at[u], sb_send.at[u], sb_recv.at[u], {"ctx": sibling})

    def key_sums(u, slot):
        sums = key_part(u, slot, e_all, x_all, w_all)
        k_rows = kv[u, 0, 2 * slot : 2 * slot + 2].reshape(2 * T, HD).astype(F32)
        k_gain_acc[...] += jnp.sum((sums[0] * k_rows).reshape(32, 8, HD), 0)
        return sums

    def reduce_start(u):
        sums = key_sums(u, 2)
        for d in range(2):
            b1_out[u, d] = sums[d].reshape(2, T, HD).astype(BF)
            b1(u, d).start()
        for d, slot in ((0, 1), (1, 3)):
            sums = key_sums(u, slot)
            for dest_core in range(2):
                b2_out[u, d, dest_core, 1 - d] = sums[1 - d][dest_core * T : dest_core * T + T].astype(BF)
                b2(u, d, dest_core, 1 - d).start()
            near_sum[u, d] = sums[d].reshape(2, T, HD)
        sums = key_sums(u, 0)
        for part in range(2):
            own_sum[u, part] = sums[part].reshape(2, T, HD)
            sib_out[u, part] = own_sum[u, part, other].astype(BF)
        sibling_sum(u).start()

    def reduce_middle(u):
        for d in range(2):
            b1(u, d).wait_recv()
            for dest_core in range(2):
                b2_out[u, d, dest_core, d] = (near_sum[u, d, dest_core] + b1_in[u, d, dest_core].astype(F32)).astype(BF)
                b2(u, d, dest_core, d).start()

    def reduce_finish(u):
        sibling_sum(u).wait_recv()
        for d in range(2):
            for src_core in range(2):
                for part in range(2):
                    b2_arrival(u, d, src_core, part).wait_recv()
        for rel in range(2):
            at = core if rel == 0 else other
            sums = []
            for part in range(2):
                own = own_sum[u, part, core] if rel == 0 else sib_in[u, part].astype(F32)
                sums.append(own + b2_in[u, 0, at, part].astype(F32) + b2_in[u, 1, at, part].astype(F32))
            cols = pl.ds(pl.multiple_of(at * 256 + u * HD, HD), HD)
            block = k_in[:, cols].astype(F32)
            factor = lax.rsqrt(jnp.mean(block * block, -1, keepdims=True) + EPS)
            unit = block * factor
            scaled = sums[0] * k_gain_row
            mean = jnp.mean(scaled * unit, -1, keepdims=True)
            dk_buf[:, cols] = (factor * (scaled - unit * mean)).astype(BF)
            dv_buf[:, cols] = sums[1].astype(BF)

    def out_local(u):
        return pltpu.make_async_copy(dq_buf.at[u, 0], dq_hbm.at[0, :, head_cols(core, u)], out_sem.at[u])

    def out_remote(u):
        return remote(dq_buf.at[u, 1], dq_hbm.at[0, :, head_cols(core, u)], ox_send.at[u], ox_recv.at[u], {"ctx": sibling})

    def out_arrival(u):
        return remote(dq_buf.at[u, 1], dq_hbm.at[0, :, head_cols(other, u)], ox_send.at[u], ox_recv.at[u], {"ctx": sibling})

    def softmax_parts(u, hook_at, hook):
        def one(r, carry):
            @pl.when(r == hook_at)
            def _():
                hook()

            softmax_part(u, r, kv, q_normed, g_cols, bias, e_all, x_all, stat, w_all)
            return carry

        lax.fori_loop(0, 8, one, 0)

    def query_parts(u, lo, hi):
        def one(r, carry):
            query_part(u, r, kt, e_all, x_all, stat, q_unit, q_factor, gain_cols, dq_buf, gain_acc)
            return carry

        lax.fori_loop(lo, hi, one, 0)

    gather_start(0)
    for u in range(2):
        for part in range(2):
            kv[u, part, core] = own_kv[2 * core + u, part]
    column = jnp.broadcast_to(q_gain[...], (HD, HD)).T
    gain_cols[...] = jnp.concatenate([column, column], 1)
    gain_acc[...] = jnp.zeros_like(gain_acc)
    k_gain_acc[...] = jnp.zeros_like(k_gain_acc)
    make_bias(bias, order, chip, core)
    prepare_rows(0, 0)
    forward(0)
    gather_start(1)
    prepare_rows(1, 0)
    prepare_rows(0, 1)
    finish_gather(0)
    softmax_parts(0, STEP_FORWARD, lambda: forward(1))
    reduce_start(0)
    query_parts(0, 0, EARLY)
    out_local(0).start()
    out_remote(0).start()
    prepare_rows(1, 1)
    finish_gather(1)
    softmax_parts(1, STEP_REDUCE, lambda: reduce_middle(0))
    reduce_start(1)
    query_parts(1, 0, 4)
    out_local(1).start()
    out_remote(1).start()

    def ga(r):
        return remote(ga_in.at[ring_at], ga_in.at[ring_at], ga_send.at[r], ga_recv.at[ring_at], ring_peer(lax.rem(ring_at + r, 16)))

    def ga_arrival(r):
        j = lax.rem(ring_at + r, 16)
        return remote(ga_in.at[j], ga_in.at[j], ga_send.at[r], ga_recv.at[j], {"ctx": sibling})

    def gb(r):
        return remote(gb_in.at[dp_xy], gb_in.at[dp_xy], gb_send.at[r], gb_recv.at[dp_xy], plane_peer(lax.rem(dp_xy + r, 16)))

    def gb_arrival(r):
        j = lax.rem(dp_xy + r, 16)
        return remote(gb_in.at[j], gb_in.at[j], gb_send.at[r], gb_recv.at[j], {"ctx": sibling})

    def for_peers(act):
        def one(r, carry):
            act(r)
            return carry

        lax.fori_loop(1, 16, one, 0)

    ga_in[ring_at, 0] = jnp.sum(gain_acc[...].T.reshape(16, 8, HD), 0)
    ga_in[ring_at, 1] = k_gain_acc[...]
    for_peers(lambda r: ga(r).start())
    reduce_middle(1)
    for_peers(lambda r: ga_arrival(r).wait_recv())
    gb_in[dp_xy] = jnp.sum(ga_in[...], 0)
    for_peers(lambda r: gb(r).start())
    reduce_finish(0)
    reduce_finish(1)
    fin_k = pltpu.make_async_copy(dk_buf, dk_hbm.at[0], fin_sem.at[0])
    fin_v = pltpu.make_async_copy(dv_buf, dv_hbm.at[0], fin_sem.at[1])
    fin_k.start()
    fin_v.start()
    for_peers(lambda r: gb_arrival(r).wait_recv())
    gains = jnp.sum(jnp.sum(gb_in[...], 0), 1, keepdims=True)
    gains_out[0:1] = gains[0]
    gains_out[1:2] = gains[1] / k_gain_row

    for u in range(2):
        for d in range(2):
            for dest_core in range(2):
                for part in range(2):
                    stage1(u, d, dest_core, part).wait_send()
                    b2(u, d, dest_core, part).wait_send()
                stage2(u, d, dest_core).wait_send()
            b1(u, d).wait_send()
        sibling_kv(u).wait_send()
        sibling_sum(u).wait_send()
        for c in q_exchange(u):
            c.wait_send()
        out_local(u).wait()
        out_remote(u).wait_send()
        out_arrival(u).wait_recv()
    for_peers(lambda r: ga(r).wait_send())
    for_peers(lambda r: gb(r).wait_send())
    fin_k.wait()
    fin_v.wait()


def settle(dq, dk, dv, gains, dq_out, dk_out, dv_out, q_gain_out, k_gain_out, dq_mid, dk_mid, dv_mid, gains_mid, in_sem, out_sem):
    parts = [(gains, gains_mid), (dk, dk_mid), (dv, dv_mid)]
    outs = [(gains_mid.at[0], q_gain_out), (gains_mid.at[1], k_gain_out), (dk_mid, dk_out), (dv_mid, dv_out)]
    for i in range(4):
        rows = pl.ds(i * 32, 32)
        parts.append((dq.at[0, rows], dq_mid.at[0, rows]))
        outs.append((dq_mid.at[0, rows], dq_out.at[0, rows]))
    loads = [pltpu.make_async_copy(a, b, in_sem.at[i]) for i, (a, b) in enumerate(parts)]
    stores = [pltpu.make_async_copy(a, b, out_sem.at[i]) for i, (a, b) in enumerate(outs)]
    for c in loads:
        c.start()
    loads[0].wait()
    stores[0].start()
    for i in range(1, 7):
        loads[i].wait()
        stores[i + 1].start()
    stores[1].start()
    for c in stores:
        c.wait()


def on_device(queries, keys, values, q_gain, k_gain, out_grad, block_order):
    hbm = pl.BlockSpec(memory_space=pl.ANY)
    vmem = pl.BlockSpec(memory_space=pltpu.VMEM)
    smem = pl.BlockSpec(memory_space=pltpu.SMEM)
    dma = pltpu.SemaphoreType.DMA
    sends = [dma((2, 2)), dma((2, 2, 2, 2)), dma((2, 2, 2)), dma((2,)), dma((2, 2)), dma((2, 2, 2, 2)), dma((2,))]
    results = pl.pallas_call(
        kernel,
        out_shape=(
            jax.ShapeDtypeStruct(queries.shape, BF),
            jax.ShapeDtypeStruct(keys.shape, BF),
            jax.ShapeDtypeStruct(values.shape, BF),
            jax.ShapeDtypeStruct((2, HD), F32),
        ),
        in_specs=[smem, hbm, hbm, hbm, vmem, vmem, hbm],
        out_specs=(hbm, hbm, hbm, vmem),
        scratch_shapes=[
            pltpu.VMEM((T, HK * HD), BF),
            pltpu.VMEM((T, HK * HD), BF),
            pltpu.VMEM((2, 2, T, 1024), BF),
            pltpu.VMEM((2, 2, T, 1024), BF),
            pltpu.VMEM((2, HD, ROWS), BF),
            pltpu.VMEM((2, HD, ROWS), BF),
            pltpu.VMEM((2, HD, ROWS), F32),
            pltpu.VMEM((2, 8, ROWS), F32),
            pltpu.VMEM((HD, 256), F32),
            pltpu.VMEM((HK, 2, T, HD), BF),
            pltpu.VMEM((2, 2, 8, T, HD), BF),
            pltpu.VMEM((2, HD, KEYS), BF),
            pltpu.VMEM((2, 8, T, T), F32),
            pltpu.VMEM((2, KEYS, ROWS), BF),
            pltpu.VMEM((2, KEYS, ROWS), BF),
            pltpu.VMEM((2, 2, 8, ROWS), F32),
            pltpu.VMEM((2, 3 * HD, ROWS), BF),
            pltpu.VMEM((2, 2, 2, T, HD), F32),
            pltpu.VMEM((2, 2, 2, T, HD), F32),
            pltpu.VMEM((2, 2, T, 1024), BF),
            pltpu.VMEM((HD, HD), F32),
            pltpu.VMEM((8, HD), F32),
            pltpu.VMEM((2, 2, 2, T, HD), BF),
            pltpu.VMEM((2, 2, 2, T, HD), BF),
            pltpu.VMEM((2, 2, 2, 2, T, HD), BF),
            pltpu.VMEM((2, 2, 2, 2, T, HD), BF),
            pltpu.VMEM((2, 2, T, HD), BF),
            pltpu.VMEM((2, 2, T, HD), BF),
            pltpu.VMEM((T, HK * HD), BF),
            pltpu.VMEM((T, HK * HD), BF),
            pltpu.VMEM((16, 2, 8, HD), F32),
            pltpu.VMEM((16, 2, 8, HD), F32),
            dma((6,)),
        ]
        + [s for s in sends for _ in range(2)]
        + [dma((2,)), dma((2,)), dma((2,))]
        + [dma((16,)) for _ in range(4)]
        + [dma((2,))],
        compiler_params=pltpu.CompilerParams(
            collective_id=0, has_side_effects=True, vmem_limit_bytes=60 * 1024 * 1024
        ),
    )(block_order, queries, keys, values, q_gain.reshape(1, HD), k_gain.reshape(1, HD), out_grad)
    return pl.pallas_call(
        settle,
        out_shape=(
            jax.ShapeDtypeStruct(queries.shape, BF),
            jax.ShapeDtypeStruct(keys.shape, BF),
            jax.ShapeDtypeStruct(values.shape, BF),
            jax.ShapeDtypeStruct((HD,), F32),
            jax.ShapeDtypeStruct((HD,), F32),
        ),
        in_specs=[hbm] * 4,
        out_specs=(hbm,) * 5,
        scratch_shapes=[
            pltpu.VMEM((1, T, 32 * HD), BF),
            pltpu.VMEM((1, T, HK * HD), BF),
            pltpu.VMEM((1, T, HK * HD), BF),
            pltpu.VMEM((2, HD), F32),
            dma((7,)),
            dma((8,)),
        ],
        compiler_params=pltpu.CompilerParams(vmem_limit_bytes=60 * 1024 * 1024),
    )(*results)


def solution(mesh):
    placed = (
        P("dp", "ctx", None),
        P("dp", "ctx", None),
        P("dp", "ctx", None),
        P(),
        P(),
        P("dp", "ctx", None),
        P("dp", None),
    )
    return jax.shard_map(
        on_device,
        mesh=mesh,
        in_specs=placed,
        out_specs=(P("dp", "ctx", None), P("dp", "ctx", None), P("dp", "ctx", None), P(), P()),
        check_vma=False,
    )
```

```python
import functools
import math

import jax
import jax.numpy as jnp
from jax import lax
from jax.experimental import pallas as pl
from jax.experimental.pallas import tpu as pltpu
from jax.sharding import PartitionSpec as P

HK = 4
HD = 128
T = 128
KEYS = 8 * T
ROWS = 16 * T
EPS = 1e-06
SCALE = 1.0 / math.sqrt(HD)
EXP2_SCALE = SCALE * math.log2(math.e)
NEG = -1e30
BF = jnp.bfloat16
F32 = jnp.float32
MESH = pl.DeviceIdType.MESH
NT = (((1,), (1,)), ((), ()))
NN = (((1,), (0,)), ((), ()))

STEPS_FORWARD = (4, 7)
STEPS_REDUCE = (4, 7)


def dot(a, b, dims):
    return lax.dot_general(a, b, dims, preferred_element_type=F32)


def make_bias(bias, order, chip, core):
    keys_at = lax.broadcasted_iota(jnp.int32, (T, T), 0)
    rows_at = lax.broadcasted_iota(jnp.int32, (T, T), 1)
    for rel in range(2):
        own = order[0, 2 * chip + (core if rel == 0 else 1 - core)]
        for j in range(8):
            block = order[0, 2 * lax.rem(chip + j // 2, 4) + j % 2]
            bias[rel, j] = jnp.where(block * T + keys_at <= own * T + rows_at, 0.0, NEG)


def prepare(u, rel, hp, q_buf, g_buf, q_normed, g_cols, q_unit, q_factor, gain_cols):
    cols = pl.ds(pl.multiple_of(hp * 256, 256), 256)
    out = pl.ds(pl.multiple_of(rel * 1024 + hp * 256, 256), 256)
    q2 = q_buf[u, rel, :, cols].astype(F32)
    g2 = g_buf[u, rel, :, cols].astype(F32)
    q = jnp.concatenate([q2[:, :HD].T, q2[:, HD:].T], 1)
    factor = lax.rsqrt(jnp.mean(q * q, 0, keepdims=True) + EPS)
    unit = q * factor
    q_factor[u, :, out] = jnp.broadcast_to(factor, (8, 256))
    q_unit[u, :, out] = unit
    q_normed[u, :, out] = (unit * gain_cols[...]).astype(BF)
    g_cols[u, :, out] = jnp.concatenate([g2[:, :HD].T, g2[:, HD:].T], 1).astype(BF)


def softmax_part(u, r, kv, q_normed, g_cols, bias, e_all, x_all, stat, w_all):
    rel = r // 4
    cols = pl.ds(pl.multiple_of(r * 256, 256), 256)
    qn = q_normed[u, :, cols]
    g = g_cols[u, :, cols]
    total = jnp.zeros((8, 256), F32)
    cross = jnp.zeros((8, 256), F32)
    half = T // 2
    for j in range(0, 8, 2):
        s = dot(kv[u, 0, j : j + 2].reshape(2 * T, HD), qn, NN)
        d = dot(kv[u, 1, j : j + 2].reshape(2 * T, HD), g, NN)
        for b in range(4):
            at, row = b * half, j * T + b * half
            tile = bias[rel, j + b // 2, (b % 2) * half : (b % 2 + 1) * half, :]
            tile = jnp.concatenate([tile, tile], 1)
            e = jnp.exp2(s[at : at + half] * EXP2_SCALE + tile)
            x = e * d[at : at + half]
            total = total + jnp.sum(e.reshape(half // 8, 8, 256), 0)
            cross = cross + jnp.sum(x.reshape(half // 8, 8, 256), 0)
            e_all[u, row : row + half, cols] = e.astype(BF)
            x_all[u, row : row + half, cols] = x.astype(BF)
    inv = 1.0 / jnp.sum(total, 0, keepdims=True)
    row_dots = jnp.sum(cross, 0, keepdims=True) * inv
    stat[u, 0, :, cols] = jnp.broadcast_to(inv * SCALE, (8, 256))
    stat[u, 1, :, cols] = jnp.broadcast_to(row_dots, (8, 256))
    scaled = qn.astype(F32) * inv
    w_all[u, 0:128, cols] = (g.astype(F32) * inv).astype(BF)
    w_all[u, 128:256, cols] = (scaled * -row_dots).astype(BF)
    w_all[u, 256:384, cols] = scaled.astype(BF)


def key_part(u, slot, e_all, x_all, w_all):
    at = slice(slot * 256, slot * 256 + 256)
    both = dot(e_all[u, at, :], w_all[u, 0:256, :], NT)
    dk = (both[:, HD:] + dot(x_all[u, at, :], w_all[u, 256:384, :], NT)) * SCALE
    return dk, both[:, :HD]


def query_part(u, r, kt, e_all, x_all, stat, q_unit, q_factor, gain_cols, dq_buf):
    rel = r // 2
    rows = pl.ds(pl.multiple_of(r * 512, 512), 512)
    x = dot(kt[u], x_all[u, :, rows], NN)
    e = dot(kt[u], e_all[u, :, rows], NN)
    dq = (x - e * stat[u, 1, 0:1, rows]) * stat[u, 0, 0:1, rows]
    unit = q_unit[u, :, rows]
    gain = gain_cols[...]
    scaled = dq * jnp.concatenate([gain, gain], 1)
    mean = jnp.mean(scaled * unit, 0, keepdims=True)
    out = q_factor[u, 0:1, rows] * (scaled - unit * mean)
    cols = pl.ds(pl.multiple_of((r % 2) * 512, 512), 512)
    dq_buf[u, rel, :, cols] = jnp.concatenate([out[:, i * HD : i * HD + HD].T for i in range(4)], 1).astype(BF)


def kernel(
    order_hbm,
    q_hbm,
    k_hbm,
    v_hbm,
    q_gain_hbm,
    k_gain_hbm,
    g_hbm,
    dq_hbm,
    dk_hbm,
    dv_hbm,
    gains_hbm,
    order,
    q_gain,
    k_gain,
    gains_out,
    k_in,
    v_in,
    q_buf,
    g_buf,
    q_normed,
    g_cols,
    q_unit,
    q_factor,
    gain_cols,
    own_kv,
    kv,
    kt,
    bias,
    e_all,
    x_all,
    stat,
    w_all,
    near_sum,
    own_sum,
    dq_buf,
    gain_acc,
    b1_out,
    b1_in,
    b2_out,
    b2_in,
    sib_out,
    sib_in,
    dk_buf,
    dv_buf,
    ga_in,
    gb_in,
    load_sem,
    qx_send,
    qx_recv,
    s1_send,
    s1_recv,
    s2_send,
    s2_recv,
    sk_send,
    sk_recv,
    b1_send,
    b1_recv,
    b2_send,
    b2_recv,
    sb_send,
    sb_recv,
    out_sem,
    ox_send,
    ox_recv,
    ga_send,
    ga_recv,
    gb_send,
    gb_recv,
    fin_sem,
):
    ctx = lax.axis_index("ctx")
    dp = lax.axis_index("dp")
    chip = ctx // 2
    core = ctx % 2
    other = 1 - core
    sibling = 2 * chip + other
    near = (lax.rem(chip + 1, 4), lax.rem(chip + 3, 4))
    dp_z = dp % 2
    dp_xy = dp // 2
    ring_at = dp_z * 8 + ctx

    def ring_peer(m):
        return {"dp": dp_xy * 2 + m // 8, "ctx": m % 8}

    def plane_peer(m):
        return {"dp": m * 2 + dp_z}

    def remote(src, dst, ssem, rsem, dev):
        return pltpu.make_async_remote_copy(
            src_ref=src, dst_ref=dst, send_sem=ssem, recv_sem=rsem, device_id=dev, device_id_type=MESH
        )

    def head_cols(core_at, u):
        return pl.ds(pl.multiple_of(core_at * 2048 + u * 1024, 1024), 1024)

    barrier = pltpu.get_barrier_semaphore()

    def greet(r, carry):
        pl.semaphore_signal(barrier, inc=1, device_id=ring_peer(lax.rem(ring_at + r, 16)), device_id_type=MESH)
        pl.semaphore_signal(barrier, inc=1, device_id=plane_peer(lax.rem(dp_xy + r, 16)), device_id_type=MESH)
        return carry

    lax.fori_loop(1, 16, greet, 0)
    loads = [
        pltpu.make_async_copy(k_hbm.at[0], k_in, load_sem.at[0]),
        pltpu.make_async_copy(k_gain_hbm, k_gain, load_sem.at[6]),
        pltpu.make_async_copy(v_hbm.at[0], v_in, load_sem.at[1]),
        pltpu.make_async_copy(q_gain_hbm, q_gain, load_sem.at[7]),
        pltpu.make_async_copy(order_hbm, order, load_sem.at[8]),
    ]
    for c in loads:
        c.start()
    load_q = []
    for u in range(2):
        pair = (
            pltpu.make_async_copy(q_hbm.at[0, :, head_cols(core, u)], q_buf.at[u, 0], load_sem.at[2 + 2 * u]),
            pltpu.make_async_copy(g_hbm.at[0, :, head_cols(core, u)], g_buf.at[u, 0], load_sem.at[3 + 2 * u]),
        )
        load_q.append(pair)
        for c in pair:
            c.start()

    for c in loads:
        c.wait()
    k_gain_row = k_gain[...]
    for h in range(HK):
        block = k_in[:, h * HD : (h + 1) * HD].astype(F32)
        factor = lax.rsqrt(jnp.mean(block * block, -1, keepdims=True) + EPS)
        own_kv[h, 0] = (block * factor * k_gain_row).astype(BF)
        own_kv[h, 1] = v_in[:, h * HD : (h + 1) * HD]

    pl.semaphore_wait(barrier, 30)

    lands = (3, 1)

    def stage1(u, d, dest_core, part):
        return remote(
            own_kv.at[2 * dest_core + u, part],
            kv.at[u, part, 2 * lands[d] + core],
            s1_send.at[u, d, dest_core, part],
            s1_recv.at[u, d, core, part],
            {"ctx": 2 * near[d] + dest_core},
        )

    def stage1_arrival(u, d, src_core, part):
        at = kv.at[u, part, 2 * lands[d] + src_core]
        return remote(at, at, s1_send.at[u, d, src_core, part], s1_recv.at[u, d, src_core, part], {"ctx": sibling})

    def sibling_kv(u):
        return remote(own_kv.at[2 * other + u], kv.at[u, :, core], sk_send.at[u], sk_recv.at[u], {"ctx": sibling})

    def sibling_kv_arrival(u):
        return remote(own_kv.at[2 * core + u], kv.at[u, :, other], sk_send.at[u], sk_recv.at[u], {"ctx": sibling})

    def stage2(u, d, src_core):
        return remote(
            kv.at[u, d, 2 * lands[d] + src_core],
            kv.at[u, d, 4 + src_core],
            s2_send.at[u, d, src_core],
            s2_recv.at[u, d, src_core],
            {"ctx": 2 * near[d] + core},
        )

    def stage2_arrival(u, d, src_core):
        at = kv.at[u, d, 4 + src_core]
        return remote(at, at, s2_send.at[u, d, src_core], s2_recv.at[u, d, src_core], {"ctx": sibling})

    def q_exchange(u):
        return (
            remote(q_hbm.at[0, :, head_cols(other, u)], q_buf.at[u, 1], qx_send.at[u, 0], qx_recv.at[u, 0], {"ctx": sibling}),
            remote(g_hbm.at[0, :, head_cols(other, u)], g_buf.at[u, 1], qx_send.at[u, 1], qx_recv.at[u, 1], {"ctx": sibling}),
        )

    by_core = (core, other)

    def share(u):
        sibling_kv(u).start()
        for c in q_exchange(u):
            c.start()

    def gather_start(u):
        for first in range(2):
            for dest_core in by_core:
                for d in range(2):
                    stage1(u, d, dest_core, d if first == 0 else 1 - d).start()

    def forward(u, src_core):
        for d in range(2):
            stage1_arrival(u, d, src_core, d).wait_recv()
            stage2(u, d, src_core).start()

    def finish_gather(u):
        for src_core in range(2):
            for d in range(2):
                stage1_arrival(u, d, src_core, 1 - d).wait_recv()
        sibling_kv_arrival(u).wait_recv()
        for src_core in range(2):
            for d in range(2):
                stage2_arrival(u, d, src_core).wait_recv()
        kt[u] = kv[u, 0].reshape(KEYS, HD).T

    def prepare_rows(u, rel):
        if rel == 0:
            for c in load_q[u]:
                c.wait()
        else:
            for c in q_exchange(u):
                c.wait_recv()

        def one(hp, carry):
            prepare(u, rel, hp, q_buf, g_buf, q_normed, g_cols, q_unit, q_factor, gain_cols)
            return carry

        lax.fori_loop(0, 4, one, 0)

    def b1(u, d, kk):
        return remote(
            b1_out.at[u, d, kk], b1_in.at[u, d, kk], b1_send.at[u, d, kk], b1_recv.at[u, d, kk], {"ctx": 2 * near[d] + core}
        )

    def b2(u, d, dest_core, part):
        return remote(
            b2_out.at[u, d, dest_core, part],
            b2_in.at[u, d, core, part],
            b2_send.at[u, d, dest_core, part],
            b2_recv.at[u, d, core, part],
            {"ctx": 2 * near[d] + dest_core},
        )

    def b2_arrival(u, d, src_core, part):
        at = b2_in.at[u, d, src_core, part]
        return remote(at, at, b2_send.at[u, d, src_core, part], b2_recv.at[u, d, src_core, part], {"ctx": sibling})

    def sibling_sum(u):
        return remote(sib_out.at[u], sib_in.at[u], sb_send.at[u], sb_recv.at[u], {"ctx": sibling})

    def key_sums(u, slot):
        sums = key_part(u, slot, e_all, x_all, w_all)
        k_rows = kv[u, 0, 2 * slot : 2 * slot + 2].reshape(2 * T, HD).astype(F32)
        gain_acc[...] += jnp.sum((sums[0] * k_rows).reshape(32, 8, HD), 0)
        return sums

    def reduce_start(u):
        sums = key_sums(u, 2)
        for d in range(2):
            b1_out[u, d] = sums[d].reshape(2, T, HD).astype(BF)
        for kk in range(2):
            for d in range(2):
                b1(u, d, kk).start()
        for d, slot in ((0, 1), (1, 3)):
            sums = key_sums(u, slot)
            for dest_core in range(2):
                b2_out[u, d, dest_core, 1 - d] = sums[1 - d][dest_core * T : dest_core * T + T].astype(BF)
                b2(u, d, dest_core, 1 - d).start()
            near_sum[u, d] = sums[d].reshape(2, T, HD)
        sums = key_sums(u, 0)
        for part in range(2):
            own_sum[u, part] = sums[part].reshape(2, T, HD)
            sib_out[u, part] = own_sum[u, part, other].astype(BF)
        sibling_sum(u).start()

    def reduce_middle(u, kk):
        for d in range(2):
            b1(u, d, kk).wait_recv()
            b2_out[u, d, kk, d] = (near_sum[u, d, kk] + b1_in[u, d, kk].astype(F32)).astype(BF)
            b2(u, d, kk, d).start()

    def reduce_finish(u):
        sibling_sum(u).wait_recv()
        for d in range(2):
            for src_core in range(2):
                for part in range(2):
                    b2_arrival(u, d, src_core, part).wait_recv()
        for rel in range(2):
            at = core if rel == 0 else other
            sums = []
            for part in range(2):
                own = own_sum[u, part, core] if rel == 0 else sib_in[u, part].astype(F32)
                sums.append(own + b2_in[u, 0, at, part].astype(F32) + b2_in[u, 1, at, part].astype(F32))
            cols = pl.ds(pl.multiple_of(at * 256 + u * HD, HD), HD)
            block = k_in[:, cols].astype(F32)
            factor = lax.rsqrt(jnp.mean(block * block, -1, keepdims=True) + EPS)
            unit = block * factor
            scaled = sums[0] * k_gain_row
            mean = jnp.mean(scaled * unit, -1, keepdims=True)
            dk_buf[:, cols] = (factor * (scaled - unit * mean)).astype(BF)
            dv_buf[:, cols] = sums[1].astype(BF)

    def out_local(u):
        return pltpu.make_async_copy(dq_buf.at[u, 0], dq_hbm.at[0, :, head_cols(core, u)], out_sem.at[u])

    def out_remote(u):
        return remote(dq_buf.at[u, 1], dq_hbm.at[0, :, head_cols(core, u)], ox_send.at[u], ox_recv.at[u], {"ctx": sibling})

    def out_arrival(u):
        return remote(dq_buf.at[u, 1], dq_hbm.at[0, :, head_cols(other, u)], ox_send.at[u], ox_recv.at[u], {"ctx": sibling})

    def softmax_parts(u, hooks):
        def one(r, carry):
            for at, hook in hooks.items():
                pl.when(r == at)(hook)

            softmax_part(u, r, kv, q_normed, g_cols, bias, e_all, x_all, stat, w_all)
            return carry

        lax.fori_loop(0, 8, one, 0)

    def query_parts(u, lo, hi):
        def one(r, carry):
            query_part(u, r, kt, e_all, x_all, stat, q_unit, q_factor, gain_cols, dq_buf)
            return carry

        lax.fori_loop(lo, hi, one, 0)

    gather_start(0)
    share(0)
    share(1)
    for u in range(2):
        for part in range(2):
            kv[u, part, core] = own_kv[2 * core + u, part]
    column = jnp.broadcast_to(q_gain[...], (HD, HD)).T
    gain_cols[...] = jnp.concatenate([column, column], 1)
    gain_acc[...] = jnp.zeros_like(gain_acc)
    make_bias(bias, order, chip, core)
    prepare_rows(0, 0)
    for at in by_core:
        forward(0, at)
    gather_start(1)
    prepare_rows(1, 0)
    prepare_rows(0, 1)
    prepare_rows(1, 1)
    finish_gather(0)
    softmax_parts(0, {at: functools.partial(forward, 1, k) for at, k in zip(STEPS_FORWARD, by_core)})
    reduce_start(0)
    query_parts(0, 0, 4)
    out_local(0).start()
    out_remote(0).start()
    finish_gather(1)
    softmax_parts(1, {at: functools.partial(reduce_middle, 0, k) for at, k in zip(STEPS_REDUCE, range(2))})
    reduce_start(1)

    def ga(r):
        return remote(ga_in.at[ring_at], ga_in.at[ring_at], ga_send.at[r], ga_recv.at[ring_at], ring_peer(lax.rem(ring_at + r, 16)))

    def ga_arrival(r):
        j = lax.rem(ring_at + r, 16)
        return remote(ga_in.at[j], ga_in.at[j], ga_send.at[r], ga_recv.at[j], {"ctx": sibling})

    def gb(r):
        return remote(gb_in.at[dp_xy], gb_in.at[dp_xy], gb_send.at[r], gb_recv.at[dp_xy], plane_peer(lax.rem(dp_xy + r, 16)))

    def gb_arrival(r):
        j = lax.rem(dp_xy + r, 16)
        return remote(gb_in.at[j], gb_in.at[j], gb_send.at[r], gb_recv.at[j], {"ctx": sibling})

    def for_peers(act):
        def one(r, carry):
            act(r)
            return carry

        lax.fori_loop(1, 16, one, 0)

    gb_in[dp_xy] = jnp.sum(gain_acc[...], 0, keepdims=True)
    for_peers(lambda r: gb(r).start())
    query_parts(1, 0, 4)
    out_local(1).start()
    out_remote(1).start()
    for_peers(lambda r: gb_arrival(r).wait_recv())
    ga_in[ring_at] = jnp.sum(gb_in[...], 0)
    for_peers(lambda r: ga(r).start())
    for kk in range(2):
        reduce_middle(1, kk)
    reduce_finish(0)
    reduce_finish(1)
    fin_k = pltpu.make_async_copy(dk_buf, dk_hbm.at[0], fin_sem.at[0])
    fin_v = pltpu.make_async_copy(dv_buf, dv_hbm.at[0], fin_sem.at[1])
    fin_k.start()
    fin_v.start()
    for_peers(lambda r: ga_arrival(r).wait_recv())
    gain_sum = jnp.sum(ga_in[...], 0)
    gains_out[0:1] = gain_sum / q_gain[...]
    gains_out[1:2] = gain_sum / k_gain_row
    fin_g = pltpu.make_async_copy(gains_out, gains_hbm, fin_sem.at[2])
    fin_g.start()

    for u in range(2):
        for d in range(2):
            for dest_core in range(2):
                for part in range(2):
                    stage1(u, d, dest_core, part).wait_send()
                    b2(u, d, dest_core, part).wait_send()
                stage2(u, d, dest_core).wait_send()
            for kk in range(2):
                b1(u, d, kk).wait_send()
        sibling_kv(u).wait_send()
        sibling_sum(u).wait_send()
        for c in q_exchange(u):
            c.wait_send()
        out_local(u).wait()
        out_remote(u).wait_send()
        out_arrival(u).wait_recv()
    for_peers(lambda r: ga(r).wait_send())
    for_peers(lambda r: gb(r).wait_send())
    fin_k.wait()
    fin_v.wait()
    fin_g.wait()


def settle(dq, dk, dv, gains, dq_out, dk_out, dv_out, q_gain_out, k_gain_out, sems):
    pairs = [(gains.at[0], q_gain_out), (gains.at[1], k_gain_out), (dk, dk_out), (dv, dv_out)]
    for i in range(4):
        rows = pl.ds(i * 32, 32)
        pairs.append((dq.at[0, rows], dq_out.at[0, rows]))
    copies = [pltpu.make_async_copy(a, b, sems.at[i]) for i, (a, b) in enumerate(pairs)]
    for c in copies:
        c.start()
    for c in copies:
        c.wait()


def on_device(queries, keys, values, q_gain, k_gain, out_grad, block_order):
    hbm = pl.BlockSpec(memory_space=pl.ANY)
    dma = pltpu.SemaphoreType.DMA
    sends = [dma((2, 2)), dma((2, 2, 2, 2)), dma((2, 2, 2)), dma((2,)), dma((2, 2, 2)), dma((2, 2, 2, 2)), dma((2,))]
    operands = (block_order, queries, keys, values, q_gain.reshape(1, HD), k_gain.reshape(1, HD), out_grad)
    results = pl.pallas_call(
        kernel,
        out_shape=(
            jax.ShapeDtypeStruct(queries.shape, BF),
            jax.ShapeDtypeStruct(keys.shape, BF),
            jax.ShapeDtypeStruct(values.shape, BF),
            jax.ShapeDtypeStruct((2, HD), F32),
        ),
        in_specs=[pl.BlockSpec(memory_space=pltpu.HBM)] * 7,
        out_specs=(hbm,) * 4,
        scratch_shapes=[
            pltpu.SMEM((1, 8), jnp.int32),
            pltpu.VMEM((1, HD), F32),
            pltpu.VMEM((1, HD), F32),
            pltpu.VMEM((2, HD), F32),
            pltpu.VMEM((T, HK * HD), BF),
            pltpu.VMEM((T, HK * HD), BF),
            pltpu.VMEM((2, 2, T, 1024), BF),
            pltpu.VMEM((2, 2, T, 1024), BF),
            pltpu.VMEM((2, HD, ROWS), BF),
            pltpu.VMEM((2, HD, ROWS), BF),
            pltpu.VMEM((2, HD, ROWS), F32),
            pltpu.VMEM((2, 8, ROWS), F32),
            pltpu.VMEM((HD, 256), F32),
            pltpu.VMEM((HK, 2, T, HD), BF),
            pltpu.VMEM((2, 2, 8, T, HD), BF),
            pltpu.VMEM((2, HD, KEYS), BF),
            pltpu.VMEM((2, 8, T, T), F32),
            pltpu.VMEM((2, KEYS, ROWS), BF),
            pltpu.VMEM((2, KEYS, ROWS), BF),
            pltpu.VMEM((2, 2, 8, ROWS), F32),
            pltpu.VMEM((2, 3 * HD, ROWS), BF),
            pltpu.VMEM((2, 2, 2, T, HD), F32),
            pltpu.VMEM((2, 2, 2, T, HD), F32),
            pltpu.VMEM((2, 2, T, 1024), BF),
            pltpu.VMEM((8, HD), F32),
            pltpu.VMEM((2, 2, 2, T, HD), BF),
            pltpu.VMEM((2, 2, 2, T, HD), BF),
            pltpu.VMEM((2, 2, 2, 2, T, HD), BF),
            pltpu.VMEM((2, 2, 2, 2, T, HD), BF),
            pltpu.VMEM((2, 2, T, HD), BF),
            pltpu.VMEM((2, 2, T, HD), BF),
            pltpu.VMEM((T, HK * HD), BF),
            pltpu.VMEM((T, HK * HD), BF),
            pltpu.VMEM((16, 1, HD), F32),
            pltpu.VMEM((16, 1, HD), F32),
            dma((9,)),
        ]
        + [s for s in sends for _ in range(2)]
        + [dma((2,)), dma((2,)), dma((2,))]
        + [dma((16,)) for _ in range(4)]
        + [dma((3,))],
        compiler_params=pltpu.CompilerParams(
            collective_id=0, has_side_effects=True, vmem_limit_bytes=44 * 1024 * 1024
        ),
    )(*(pltpu.with_memory_space_constraint(x, pltpu.HBM) for x in operands))
    return pl.pallas_call(
        settle,
        out_shape=(
            jax.ShapeDtypeStruct(queries.shape, BF),
            jax.ShapeDtypeStruct(keys.shape, BF),
            jax.ShapeDtypeStruct(values.shape, BF),
            jax.ShapeDtypeStruct((HD,), F32),
            jax.ShapeDtypeStruct((HD,), F32),
        ),
        in_specs=[hbm] * 4,
        out_specs=(hbm,) * 5,
        scratch_shapes=[dma((8,))],
        compiler_params=pltpu.CompilerParams(vmem_limit_bytes=16 * 1024 * 1024),
    )(*results)


def solution(mesh):
    placed = (
        P("dp", "ctx", None),
        P("dp", "ctx", None),
        P("dp", "ctx", None),
        P(),
        P(),
        P("dp", "ctx", None),
        P("dp", None),
    )
    return jax.shard_map(
        on_device,
        mesh=mesh,
        in_specs=placed,
        out_specs=(P("dp", "ctx", None), P("dp", "ctx", None), P("dp", "ctx", None), P(), P()),
        check_vma=False,
    )
```

```python
import math

import jax
import jax.numpy as jnp
from jax import lax
from jax.experimental import pallas as pl
from jax.experimental.pallas import tpu as pltpu
from jax.sharding import PartitionSpec as P

HK = 4
HD = 128
T = 128
KEYS = 8 * T
ROWS = 16 * T
EPS = 1e-06
SCALE = 1.0 / math.sqrt(HD)
EXP2_SCALE = SCALE * math.log2(math.e)
NEG = -1e30
BF = jnp.bfloat16
F32 = jnp.float32
MESH = pl.DeviceIdType.MESH
NT = (((1,), (1,)), ((), ()))
NN = (((1,), (0,)), ((), ()))

NEAR_SLOTS = (0, 1, 3)
FAR_SLOTS = (2,)


def dot(a, b, dims):
    return lax.dot_general(a, b, dims, preferred_element_type=F32)


def make_bias(bias, order, chip, core):
    keys_at = lax.broadcasted_iota(jnp.int32, (T, T), 0)
    rows_at = lax.broadcasted_iota(jnp.int32, (T, T), 1)
    for rel in range(2):
        own = order[0, 2 * chip + (core if rel == 0 else 1 - core)]
        for j in range(8):
            block = order[0, 2 * lax.rem(chip + j // 2, 4) + j % 2]
            bias[rel, j] = jnp.where(block * T + keys_at <= own * T + rows_at, 0.0, NEG)


def prepare(u, rel, hp, q_buf, g_buf, q_normed, g_cols, q_unit, q_factor, gain_cols):
    cols = pl.ds(pl.multiple_of(hp * 256, 256), 256)
    out = pl.ds(pl.multiple_of(rel * 1024 + hp * 256, 256), 256)
    q2 = q_buf[u, rel, :, cols].astype(F32)
    g2 = g_buf[u, rel, :, cols].astype(F32)
    q = jnp.concatenate([q2[:, :HD].T, q2[:, HD:].T], 1)
    factor = lax.rsqrt(jnp.mean(q * q, 0, keepdims=True) + EPS)
    unit = q * factor
    q_factor[u, :, out] = jnp.broadcast_to(factor, (8, 256))
    q_unit[u, :, out] = unit
    q_normed[u, :, out] = (unit * gain_cols[...]).astype(BF)
    g_cols[u, :, out] = jnp.concatenate([g2[:, :HD].T, g2[:, HD:].T], 1).astype(BF)


def softmax_part(u, r, slots, kv, q_normed, g_cols, bias, e_all, x_all, sums, stat, w_all):
    rel = r // 4
    cols = pl.ds(pl.multiple_of(r * 256, 256), 256)
    qn = q_normed[u, :, cols]
    g = g_cols[u, :, cols]
    first = slots == NEAR_SLOTS
    total = jnp.zeros((8, 256), F32) if first else sums[0, :, cols]
    cross = jnp.zeros((8, 256), F32) if first else sums[1, :, cols]
    half = T // 2
    for j in (2 * slot for slot in slots):
        s = dot(kv[u, 0, j : j + 2].reshape(2 * T, HD), qn, NN)
        d = dot(kv[u, 1, j : j + 2].reshape(2 * T, HD), g, NN)
        for b in range(4):
            at, row = b * half, j * T + b * half
            tile = bias[rel, j + b // 2, (b % 2) * half : (b % 2 + 1) * half, :]
            tile = jnp.concatenate([tile, tile], 1)
            e = jnp.exp2(s[at : at + half] * EXP2_SCALE + tile)
            x = e * d[at : at + half]
            total = total + jnp.sum(e.reshape(half // 8, 8, 256), 0)
            cross = cross + jnp.sum(x.reshape(half // 8, 8, 256), 0)
            e_all[u, row : row + half, cols] = e.astype(BF)
            x_all[u, row : row + half, cols] = x.astype(BF)
    if first:
        sums[0, :, cols] = total
        sums[1, :, cols] = cross
        return
    inv = 1.0 / jnp.sum(total, 0, keepdims=True)
    row_dots = jnp.sum(cross, 0, keepdims=True) * inv
    stat[u, 0, :, cols] = jnp.broadcast_to(inv * SCALE, (8, 256))
    stat[u, 1, :, cols] = jnp.broadcast_to(row_dots, (8, 256))
    scaled = qn.astype(F32) * inv
    w_all[u, 0:128, cols] = (g.astype(F32) * inv).astype(BF)
    w_all[u, 128:256, cols] = (scaled * -row_dots).astype(BF)
    w_all[u, 256:384, cols] = scaled.astype(BF)


def key_part(u, slot, e_all, x_all, w_all):
    at = slice(slot * 256, slot * 256 + 256)
    both = dot(e_all[u, at, :], w_all[u, 0:256, :], NT)
    dk = (both[:, HD:] + dot(x_all[u, at, :], w_all[u, 256:384, :], NT)) * SCALE
    return dk, both[:, :HD]


def query_part(u, r, kt, e_all, x_all, stat, q_unit, q_factor, gain_cols, dq_buf):
    rel = r
    rows = pl.ds(pl.multiple_of(r * 1024, 1024), 1024)
    x = dot(kt[u], x_all[u, :, rows], NN)
    e = dot(kt[u], e_all[u, :, rows], NN)
    dq = (x - e * stat[u, 1, 0:1, rows]) * stat[u, 0, 0:1, rows]
    unit = q_unit[u, :, rows]
    gain = gain_cols[...]
    scaled = dq * jnp.concatenate([gain] * 4, 1)
    mean = jnp.mean(scaled * unit, 0, keepdims=True)
    out = q_factor[u, 0:1, rows] * (scaled - unit * mean)
    dq_buf[u, rel] = jnp.concatenate([out[:, i * HD : i * HD + HD].T for i in range(8)], 1).astype(BF)


def kernel(
    order_hbm,
    q_hbm,
    k_hbm,
    v_hbm,
    q_gain_hbm,
    k_gain_hbm,
    g_hbm,
    dq_hbm,
    dk_hbm,
    dv_hbm,
    gains_hbm,
    order,
    q_gain,
    k_gain,
    gains_out,
    k_in,
    v_in,
    q_buf,
    g_buf,
    q_normed,
    g_cols,
    q_unit,
    q_factor,
    gain_cols,
    own_kv,
    kv,
    kt,
    bias,
    e_all,
    x_all,
    sums,
    stat,
    w_all,
    near_sum,
    own_sum,
    dq_buf,
    gain_acc,
    b1_out,
    b1_in,
    b2_out,
    b2_in,
    sib_out,
    sib_in,
    fin_sum,
    fin_factor,
    fin_unit,
    dk_buf,
    dv_buf,
    ga_in,
    gb_in,
    load_sem,
    qx_send,
    qx_recv,
    s1_send,
    s1_recv,
    s2_send,
    s2_recv,
    sk_send,
    sk_recv,
    b1_send,
    b1_recv,
    b2_send,
    b2_recv,
    sb_send,
    sb_recv,
    out_sem,
    ox_send,
    ox_recv,
    ga_send,
    ga_recv,
    gb_send,
    gb_recv,
    fin_sem,
):
    ctx = lax.axis_index("ctx")
    dp = lax.axis_index("dp")
    chip = ctx // 2
    core = ctx % 2
    other = 1 - core
    sibling = 2 * chip + other
    near = (lax.rem(chip + 1, 4), lax.rem(chip + 3, 4))
    dp_z = dp % 2
    dp_xy = dp // 2
    ring_at = dp_z * 8 + ctx

    def ring_peer(m):
        return {"dp": dp_xy * 2 + m // 8, "ctx": m % 8}

    def plane_peer(m):
        return {"dp": m * 2 + dp_z}

    def remote(src, dst, ssem, rsem, dev):
        return pltpu.make_async_remote_copy(
            src_ref=src, dst_ref=dst, send_sem=ssem, recv_sem=rsem, device_id=dev, device_id_type=MESH
        )

    def head_cols(core_at, u):
        return pl.ds(pl.multiple_of(core_at * 2048 + u * 1024, 1024), 1024)

    barrier = pltpu.get_barrier_semaphore()

    def greet(dev):
        pl.semaphore_signal(barrier, inc=1, device_id=dev, device_id_type=MESH)

    def greet_ring(i, carry):
        greet({"dp": dp_xy * 2 + 1 - dp_z, "ctx": i})
        return carry

    def greet_plane(r, carry):
        greet(plane_peer(lax.rem(dp_xy + r, 16)))
        return carry

    for i in (near[0], near[1], lax.rem(chip + 2, 4)):
        for k in range(2):
            greet({"ctx": 2 * i + k})
    greet({"ctx": sibling})
    loads = [
        pltpu.make_async_copy(k_hbm.at[0], k_in, load_sem.at[0]),
        pltpu.make_async_copy(k_gain_hbm, k_gain, load_sem.at[6]),
        pltpu.make_async_copy(v_hbm.at[0], v_in, load_sem.at[1]),
        pltpu.make_async_copy(q_gain_hbm, q_gain, load_sem.at[7]),
        pltpu.make_async_copy(order_hbm, order, load_sem.at[8]),
    ]
    for c in loads:
        c.start()
    lax.fori_loop(0, 8, greet_ring, 0)
    lax.fori_loop(1, 16, greet_plane, 0)
    load_q = []
    for u in range(2):
        pair = (
            pltpu.make_async_copy(q_hbm.at[0, :, head_cols(core, u)], q_buf.at[u, 0], load_sem.at[2 + 2 * u]),
            pltpu.make_async_copy(g_hbm.at[0, :, head_cols(core, u)], g_buf.at[u, 0], load_sem.at[3 + 2 * u]),
        )
        load_q.append(pair)
        for c in pair:
            c.start()

    for c in loads:
        c.wait()
    k_gain_row = k_gain[...]
    for h in range(HK):
        block = k_in[:, h * HD : (h + 1) * HD].astype(F32)
        factor = lax.rsqrt(jnp.mean(block * block, -1, keepdims=True) + EPS)
        own_kv[h, 0] = (block * factor * k_gain_row).astype(BF)
        own_kv[h, 1] = v_in[:, h * HD : (h + 1) * HD]

    pl.semaphore_wait(barrier, 30)

    lands = (3, 1)

    def stage1(u, d, dest_core, part):
        return remote(
            own_kv.at[2 * dest_core + u, part],
            kv.at[u, part, 2 * lands[d] + core],
            s1_send.at[u, d, dest_core, part],
            s1_recv.at[u, d, core, part],
            {"ctx": 2 * near[d] + dest_core},
        )

    def stage1_arrival(u, d, src_core, part):
        at = kv.at[u, part, 2 * lands[d] + src_core]
        return remote(at, at, s1_send.at[u, d, src_core, part], s1_recv.at[u, d, src_core, part], {"ctx": sibling})

    def sibling_kv(u):
        return remote(own_kv.at[2 * other + u], kv.at[u, :, core], sk_send.at[u], sk_recv.at[u], {"ctx": sibling})

    def sibling_kv_arrival(u):
        return remote(own_kv.at[2 * core + u], kv.at[u, :, other], sk_send.at[u], sk_recv.at[u], {"ctx": sibling})

    def stage2(u, d, src_core):
        return remote(
            kv.at[u, d, 2 * lands[d] + src_core],
            kv.at[u, d, 4 + src_core],
            s2_send.at[u, d, src_core],
            s2_recv.at[u, d, src_core],
            {"ctx": 2 * near[d] + core},
        )

    def stage2_arrival(u, d, src_core):
        at = kv.at[u, d, 4 + src_core]
        return remote(at, at, s2_send.at[u, d, src_core], s2_recv.at[u, d, src_core], {"ctx": sibling})

    def q_exchange(u):
        return (
            remote(q_hbm.at[0, :, head_cols(other, u)], q_buf.at[u, 1], qx_send.at[u, 0], qx_recv.at[u, 0], {"ctx": sibling}),
            remote(g_hbm.at[0, :, head_cols(other, u)], g_buf.at[u, 1], qx_send.at[u, 1], qx_recv.at[u, 1], {"ctx": sibling}),
        )

    by_core = (core, other)

    def share(u):
        sibling_kv(u).start()
        for c in q_exchange(u):
            c.start()

    def gather_start(u):
        for first in range(2):
            for dest_core in by_core:
                for d in range(2):
                    stage1(u, d, dest_core, d if first == 0 else 1 - d).start()

    def forward(u, src_core):
        for d in range(2):
            stage1_arrival(u, d, src_core, d).wait_recv()
            stage2(u, d, src_core).start()

    def near_gather(u):
        for src_core in range(2):
            for d in range(2):
                stage1_arrival(u, d, src_core, 1 - d).wait_recv()
        sibling_kv_arrival(u).wait_recv()

    def far_gather(u):
        for src_core in range(2):
            for d in range(2):
                stage2_arrival(u, d, src_core).wait_recv()

    def prepare_rows(u, rel):
        if rel == 0:
            for c in load_q[u]:
                c.wait()
        else:
            for c in q_exchange(u):
                c.wait_recv()

        def one(hp, carry):
            prepare(u, rel, hp, q_buf, g_buf, q_normed, g_cols, q_unit, q_factor, gain_cols)
            return carry

        lax.fori_loop(0, 4, one, 0)

    def b1(u, d, kk):
        return remote(
            b1_out.at[u, d, kk], b1_in.at[u, d, kk], b1_send.at[u, d, kk], b1_recv.at[u, d, kk], {"ctx": 2 * near[d] + core}
        )

    def b2(u, d, dest_core, part):
        return remote(
            b2_out.at[u, d, dest_core, part],
            b2_in.at[u, d, core, part],
            b2_send.at[u, d, dest_core, part],
            b2_recv.at[u, d, core, part],
            {"ctx": 2 * near[d] + dest_core},
        )

    def b2_arrival(u, d, src_core, part):
        at = b2_in.at[u, d, src_core, part]
        return remote(at, at, b2_send.at[u, d, src_core, part], b2_recv.at[u, d, src_core, part], {"ctx": sibling})

    def sibling_sum(u):
        return remote(sib_out.at[u], sib_in.at[u], sb_send.at[u], sb_recv.at[u], {"ctx": sibling})

    def key_sums(u, slot):
        both = key_part(u, slot, e_all, x_all, w_all)
        k_rows = kv[u, 0, 2 * slot : 2 * slot + 2].reshape(2 * T, HD).astype(F32)
        gain_acc[...] += jnp.sum((both[0] * k_rows).reshape(32, 8, HD), 0)
        return [x.reshape(2, T, HD) for x in both]

    def far_sums(u):
        both = key_sums(u, 2)
        for d in range(2):
            b1_out[u, d] = both[d].astype(BF)

    def far_start(u):
        for kk in range(2):
            for d in range(2):
                b1(u, d, kk).start()

    def near_sums(u, d):
        both = key_sums(u, (1, 3)[d])
        b2_out[u, d, :, 1 - d] = both[1 - d].astype(BF)
        near_sum[u, d] = both[d]

    def near_start(u, d):
        for dest_core in range(2):
            b2(u, d, dest_core, 1 - d).start()

    def own_sums(u):
        both = key_sums(u, 0)
        for part in range(2):
            own_sum[u, part] = both[part]
            sib_out[u, part] = own_sum[u, part, other].astype(BF)
        sibling_sum(u).start()

    def reduce_middle(u, kk):
        for d in range(2):
            b1(u, d, kk).wait_recv()
            b2_out[u, d, kk, d] = (near_sum[u, d, kk] + b1_in[u, d, kk].astype(F32)).astype(BF)
            b2(u, d, kk, d).start()

    def early_finish(u):
        sibling_sum(u).wait_recv()
        for d in range(2):
            for src_core in range(2):
                b2_arrival(u, d, src_core, 1 - d).wait_recv()
        for rel in range(2):
            at = core if rel == 0 else other
            for part in range(2):
                own = own_sum[u, part, core] if rel == 0 else sib_in[u, part].astype(F32)
                fin_sum[rel, part] = own + b2_in[u, 1 - part, at, part].astype(F32)
            block = k_in[:, pl.ds(pl.multiple_of(at * 256 + u * HD, HD), HD)].astype(F32)
            factor = lax.rsqrt(jnp.mean(block * block, -1, keepdims=True) + EPS)
            fin_factor[rel] = jnp.broadcast_to(factor, (T, HD))
            fin_unit[rel] = block * factor

    def late_finish(u):
        for d in range(2):
            for src_core in range(2):
                b2_arrival(u, d, src_core, d).wait_recv()
        for rel in range(2):
            at = core if rel == 0 else other
            cols = pl.ds(pl.multiple_of(at * 256 + u * HD, HD), HD)
            unit = fin_unit[rel]
            scaled = (fin_sum[rel, 0] + b2_in[u, 0, at, 0].astype(F32)) * k_gain_row
            mean = jnp.mean(scaled * unit, -1, keepdims=True)
            dk_buf[:, cols] = (fin_factor[rel] * (scaled - unit * mean)).astype(BF)
            dv_buf[:, cols] = (fin_sum[rel, 1] + b2_in[u, 1, at, 1].astype(F32)).astype(BF)

    def out_local(u):
        return pltpu.make_async_copy(dq_buf.at[u, 0], dq_hbm.at[0, :, head_cols(core, u)], out_sem.at[u])

    def out_remote(u):
        return remote(dq_buf.at[u, 1], dq_hbm.at[0, :, head_cols(core, u)], ox_send.at[u], ox_recv.at[u], {"ctx": sibling})

    def out_arrival(u):
        return remote(dq_buf.at[u, 1], dq_hbm.at[0, :, head_cols(other, u)], ox_send.at[u], ox_recv.at[u], {"ctx": sibling})

    def softmax_parts(u, slots):
        def one(r, carry):
            softmax_part(u, r, slots, kv, q_normed, g_cols, bias, e_all, x_all, sums, stat, w_all)
            return carry

        lax.fori_loop(0, 8, one, 0)

    def query_parts(u):
        kt[u] = kv[u, 0].reshape(KEYS, HD).T

        def one(r, carry):
            query_part(u, r, kt, e_all, x_all, stat, q_unit, q_factor, gain_cols, dq_buf)
            return carry

        lax.fori_loop(0, 2, one, 0)
        out_local(u).start()
        out_remote(u).start()

    gather_start(0)
    share(0)
    share(1)
    for u in range(2):
        for part in range(2):
            kv[u, part, core] = own_kv[2 * core + u, part]
    column = jnp.broadcast_to(q_gain[...], (HD, HD)).T
    gain_cols[...] = jnp.concatenate([column, column], 1)
    gain_acc[...] = jnp.zeros_like(gain_acc)
    make_bias(bias, order, chip, core)
    prepare_rows(0, 0)
    for at in by_core:
        forward(0, at)
    gather_start(1)
    prepare_rows(0, 1)
    prepare_rows(1, 0)
    prepare_rows(1, 1)
    near_gather(0)
    softmax_parts(0, NEAR_SLOTS)
    far_gather(0)
    softmax_parts(0, FAR_SLOTS)
    far_sums(0)
    forward(1, core)
    near_sums(0, 0)
    near_sums(0, 1)
    forward(1, other)
    far_start(0)
    near_start(0, 0)
    near_start(0, 1)
    own_sums(0)
    near_gather(1)
    softmax_parts(1, NEAR_SLOTS)
    far_gather(1)
    softmax_parts(1, FAR_SLOTS)
    reduce_middle(0, 0)
    far_sums(1)
    far_start(1)
    near_sums(1, 0)
    near_start(1, 0)
    reduce_middle(0, 1)
    near_sums(1, 1)
    near_start(1, 1)
    own_sums(1)

    def ga(r):
        return remote(ga_in.at[ring_at], ga_in.at[ring_at], ga_send.at[r], ga_recv.at[ring_at], ring_peer(lax.rem(ring_at + r, 16)))

    def ga_arrival(r):
        j = lax.rem(ring_at + r, 16)
        return remote(ga_in.at[j], ga_in.at[j], ga_send.at[r], ga_recv.at[j], {"ctx": sibling})

    def gb(r):
        return remote(gb_in.at[dp_xy], gb_in.at[dp_xy], gb_send.at[r], gb_recv.at[dp_xy], plane_peer(lax.rem(dp_xy + r, 16)))

    def gb_arrival(r):
        j = lax.rem(dp_xy + r, 16)
        return remote(gb_in.at[j], gb_in.at[j], gb_send.at[r], gb_recv.at[j], {"ctx": sibling})

    def for_peers(act):
        def one(r, carry):
            act(r)
            return carry

        lax.fori_loop(1, 16, one, 0)

    gb_in[dp_xy] = jnp.sum(gain_acc[...], 0, keepdims=True)
    for_peers(lambda r: gb(r).start())
    query_parts(0)
    query_parts(1)
    for_peers(lambda r: gb_arrival(r).wait_recv())
    ga_in[ring_at] = jnp.sum(gb_in[...], 0)
    for_peers(lambda r: ga(r).start())
    for kk in range(2):
        reduce_middle(1, kk)
    early_finish(0)
    late_finish(0)
    early_finish(1)
    for u in range(2):
        for d in range(2):
            for dest_core in range(2):
                for part in range(2):
                    stage1(u, d, dest_core, part).wait_send()
                stage2(u, d, dest_core).wait_send()
                b1(u, d, dest_core).wait_send()
                b2(u, d, dest_core, 1 - d).wait_send()
                if u == 0:
                    b2(u, d, dest_core, d).wait_send()
        sibling_kv(u).wait_send()
        sibling_sum(u).wait_send()
        for c in q_exchange(u):
            c.wait_send()
        out_local(u).wait()
        out_remote(u).wait_send()
        out_arrival(u).wait_recv()
    for_peers(lambda r: gb(r).wait_send())
    for_peers(lambda r: ga(r).wait_send())
    for_peers(lambda r: ga_arrival(r).wait_recv())
    gain_sum = jnp.sum(ga_in[...], 0)
    gains_out[0:1] = gain_sum / q_gain[...]
    gains_out[1:2] = gain_sum / k_gain_row
    fin_g = pltpu.make_async_copy(gains_out, gains_hbm, fin_sem.at[2])
    fin_g.start()
    late_finish(1)
    fin_k = pltpu.make_async_copy(dk_buf, dk_hbm.at[0], fin_sem.at[0])
    fin_v = pltpu.make_async_copy(dv_buf, dv_hbm.at[0], fin_sem.at[1])
    fin_k.start()
    fin_v.start()
    for d in range(2):
        for dest_core in range(2):
            b2(1, d, dest_core, d).wait_send()
    fin_g.wait()
    fin_k.wait()
    fin_v.wait()


def settle(dq, dk, dv, gains, dq_out, dk_out, dv_out, q_gain_out, k_gain_out, sems):
    pairs = [(gains.at[0], q_gain_out), (gains.at[1], k_gain_out), (dk, dk_out), (dv, dv_out)]
    for i in range(4):
        rows = pl.ds(i * 32, 32)
        pairs.append((dq.at[0, rows], dq_out.at[0, rows]))
    copies = [pltpu.make_async_copy(a, b, sems.at[i]) for i, (a, b) in enumerate(pairs)]
    for c in copies:
        c.start()
    for c in copies:
        c.wait()


def on_device(queries, keys, values, q_gain, k_gain, out_grad, block_order):
    hbm = pl.BlockSpec(memory_space=pl.ANY)
    dma = pltpu.SemaphoreType.DMA
    sends = [dma((2, 2)), dma((2, 2, 2, 2)), dma((2, 2, 2)), dma((2,)), dma((2, 2, 2)), dma((2, 2, 2, 2)), dma((2,))]
    operands = (block_order, queries, keys, values, q_gain.reshape(1, HD), k_gain.reshape(1, HD), out_grad)
    results = pl.pallas_call(
        kernel,
        out_shape=(
            jax.ShapeDtypeStruct(queries.shape, BF),
            jax.ShapeDtypeStruct(keys.shape, BF),
            jax.ShapeDtypeStruct(values.shape, BF),
            jax.ShapeDtypeStruct((2, HD), F32),
        ),
        in_specs=[pl.BlockSpec(memory_space=pltpu.HBM)] * 7,
        out_specs=(hbm,) * 4,
        scratch_shapes=[
            pltpu.SMEM((1, 8), jnp.int32),
            pltpu.VMEM((1, HD), F32),
            pltpu.VMEM((1, HD), F32),
            pltpu.VMEM((2, HD), F32),
            pltpu.VMEM((T, HK * HD), BF),
            pltpu.VMEM((T, HK * HD), BF),
            pltpu.VMEM((2, 2, T, 1024), BF),
            pltpu.VMEM((2, 2, T, 1024), BF),
            pltpu.VMEM((2, HD, ROWS), BF),
            pltpu.VMEM((2, HD, ROWS), BF),
            pltpu.VMEM((2, HD, ROWS), F32),
            pltpu.VMEM((2, 8, ROWS), F32),
            pltpu.VMEM((HD, 256), F32),
            pltpu.VMEM((HK, 2, T, HD), BF),
            pltpu.VMEM((2, 2, 8, T, HD), BF),
            pltpu.VMEM((2, HD, KEYS), BF),
            pltpu.VMEM((2, 8, T, T), F32),
            pltpu.VMEM((2, KEYS, ROWS), BF),
            pltpu.VMEM((2, KEYS, ROWS), BF),
            pltpu.VMEM((2, 8, ROWS), F32),
            pltpu.VMEM((2, 2, 8, ROWS), F32),
            pltpu.VMEM((2, 3 * HD, ROWS), BF),
            pltpu.VMEM((2, 2, 2, T, HD), F32),
            pltpu.VMEM((2, 2, 2, T, HD), F32),
            pltpu.VMEM((2, 2, T, 1024), BF),
            pltpu.VMEM((8, HD), F32),
            pltpu.VMEM((2, 2, 2, T, HD), BF),
            pltpu.VMEM((2, 2, 2, T, HD), BF),
            pltpu.VMEM((2, 2, 2, 2, T, HD), BF),
            pltpu.VMEM((2, 2, 2, 2, T, HD), BF),
            pltpu.VMEM((2, 2, T, HD), BF),
            pltpu.VMEM((2, 2, T, HD), BF),
            pltpu.VMEM((2, 2, T, HD), F32),
            pltpu.VMEM((2, T, HD), F32),
            pltpu.VMEM((2, T, HD), F32),
            pltpu.VMEM((T, HK * HD), BF),
            pltpu.VMEM((T, HK * HD), BF),
            pltpu.VMEM((16, 1, HD), F32),
            pltpu.VMEM((16, 1, HD), F32),
            dma((9,)),
        ]
        + [s for s in sends for _ in range(2)]
        + [dma((2,)), dma((2,)), dma((2,))]
        + [dma((16,)) for _ in range(4)]
        + [dma((3,))],
        compiler_params=pltpu.CompilerParams(
            collective_id=0, has_side_effects=True, vmem_limit_bytes=44 * 1024 * 1024
        ),
    )(*(pltpu.with_memory_space_constraint(x, pltpu.HBM) for x in operands))
    return pl.pallas_call(
        settle,
        out_shape=(
            jax.ShapeDtypeStruct(queries.shape, BF),
            jax.ShapeDtypeStruct(keys.shape, BF),
            jax.ShapeDtypeStruct(values.shape, BF),
            jax.ShapeDtypeStruct((HD,), F32),
            jax.ShapeDtypeStruct((HD,), F32),
        ),
        in_specs=[hbm] * 4,
        out_specs=(hbm,) * 5,
        scratch_shapes=[dma((8,))],
        compiler_params=pltpu.CompilerParams(vmem_limit_bytes=16 * 1024 * 1024),
    )(*results)


def solution(mesh):
    placed = (
        P("dp", "ctx", None),
        P("dp", "ctx", None),
        P("dp", "ctx", None),
        P(),
        P(),
        P("dp", "ctx", None),
        P("dp", None),
    )
    return jax.shard_map(
        on_device,
        mesh=mesh,
        in_specs=placed,
        out_specs=(P("dp", "ctx", None), P("dp", "ctx", None), P("dp", "ctx", None), P(), P()),
        check_vma=False,
    )
```

```python
import math

import jax
import jax.numpy as jnp
from jax import lax
from jax.experimental import pallas as pl
from jax.experimental.pallas import tpu as pltpu
from jax.sharding import PartitionSpec as P

HK = 4
HD = 128
T = 128
KEYS = 8 * T
ROWS = 16 * T
EPS = 1e-06
SCALE = 1.0 / math.sqrt(HD)
EXP2_SCALE = SCALE * math.log2(math.e)
NEG = -1e30
BF = jnp.bfloat16
F32 = jnp.float32
MESH = pl.DeviceIdType.MESH
NT = (((1,), (1,)), ((), ()))
NN = (((1,), (0,)), ((), ()))

NEAR_SLOTS = (0, 1, 3)
FAR_SLOTS = (2,)


def dot(a, b, dims):
    return lax.dot_general(a, b, dims, preferred_element_type=F32)


def make_bias(bias, order, chip, core):
    keys_at = lax.broadcasted_iota(jnp.int32, (T, T), 0)
    rows_at = lax.broadcasted_iota(jnp.int32, (T, T), 1)
    for rel in range(2):
        own = order[0, 2 * chip + (core if rel == 0 else 1 - core)]
        for j in range(8):
            block = order[0, 2 * lax.rem(chip + j // 2, 4) + j % 2]
            bias[rel, j] = jnp.where(block * T + keys_at <= own * T + rows_at, 0.0, NEG)


def prepare(u, rel, hp, q_buf, g_buf, q_normed, g_cols, q_unit, q_factor, gain_cols):
    cols = pl.ds(pl.multiple_of(hp * 256, 256), 256)
    out = pl.ds(pl.multiple_of(rel * 1024 + hp * 256, 256), 256)
    q2 = q_buf[u, rel, :, cols].astype(F32)
    g2 = g_buf[u, rel, :, cols].astype(F32)
    q = jnp.concatenate([q2[:, :HD].T, q2[:, HD:].T], 1)
    factor = lax.rsqrt(jnp.mean(q * q, 0, keepdims=True) + EPS)
    unit = q * factor
    q_factor[u, :, out] = jnp.broadcast_to(factor, (8, 256))
    q_unit[u, :, out] = unit
    q_normed[u, :, out] = (unit * gain_cols[...]).astype(BF)
    g_cols[u, :, out] = jnp.concatenate([g2[:, :HD].T, g2[:, HD:].T], 1).astype(BF)


def softmax_part(u, r, slots, kv, q_normed, g_cols, bias, e_all, x_all, sums, stat, w_all):
    rel = r // 2
    cols = pl.ds(pl.multiple_of(r * 512, 512), 512)
    qn = q_normed[u, :, cols]
    g = g_cols[u, :, cols]
    first = slots == NEAR_SLOTS
    total = jnp.zeros((8, 512), F32) if first else sums[0, :, cols]
    cross = jnp.zeros((8, 512), F32) if first else sums[1, :, cols]
    half = T // 2
    for j in (2 * slot for slot in slots):
        s = dot(kv[u, 0, j : j + 2].reshape(2 * T, HD), qn, NN)
        d = dot(kv[u, 1, j : j + 2].reshape(2 * T, HD), g, NN)
        for b in range(4):
            at, row = b * half, j * T + b * half
            tile = bias[rel, j + b // 2, (b % 2) * half : (b % 2 + 1) * half, :]
            tile = jnp.concatenate([tile] * 4, 1)
            e = jnp.exp2(s[at : at + half] * EXP2_SCALE + tile)
            x = e * d[at : at + half]
            total = total + jnp.sum(e.reshape(half // 8, 8, 512), 0)
            cross = cross + jnp.sum(x.reshape(half // 8, 8, 512), 0)
            e_all[u, row : row + half, cols] = e.astype(BF)
            x_all[u, row : row + half, cols] = x.astype(BF)
    if first:
        sums[0, :, cols] = total
        sums[1, :, cols] = cross
        return
    inv = 1.0 / jnp.sum(total, 0, keepdims=True)
    row_dots = jnp.sum(cross, 0, keepdims=True) * inv
    stat[u, 0, :, cols] = jnp.broadcast_to(inv * SCALE, (8, 512))
    stat[u, 1, :, cols] = jnp.broadcast_to(row_dots, (8, 512))
    scaled = qn.astype(F32) * inv
    w_all[u, 0:128, cols] = (g.astype(F32) * inv).astype(BF)
    w_all[u, 128:256, cols] = (scaled * -row_dots).astype(BF)
    w_all[u, 256:384, cols] = scaled.astype(BF)


def key_part(u, slot, e_all, x_all, w_all):
    at = slice(slot * 256, slot * 256 + 256)
    both = dot(e_all[u, at, :], w_all[u, 0:256, :], NT)
    dk = (both[:, HD:] + dot(x_all[u, at, :], w_all[u, 256:384, :], NT)) * SCALE
    return dk, both[:, :HD]


def query_part(u, r, kt, e_all, x_all, stat, q_unit, q_factor, gain_cols, dq_buf):
    rel = r
    rows = pl.ds(pl.multiple_of(r * 1024, 1024), 1024)
    x = dot(kt[u], x_all[u, :, rows], NN)
    e = dot(kt[u], e_all[u, :, rows], NN)
    dq = (x - e * stat[u, 1, 0:1, rows]) * stat[u, 0, 0:1, rows]
    unit = q_unit[u, :, rows]
    gain = gain_cols[...]
    scaled = dq * jnp.concatenate([gain] * 4, 1)
    mean = jnp.mean(scaled * unit, 0, keepdims=True)
    out = q_factor[u, 0:1, rows] * (scaled - unit * mean)
    dq_buf[u, rel] = jnp.concatenate([out[:, i * HD : i * HD + HD].T for i in range(8)], 1).astype(BF)


def kernel(
    order_hbm,
    q_hbm,
    k_hbm,
    v_hbm,
    q_gain_hbm,
    k_gain_hbm,
    g_hbm,
    dq_hbm,
    dk_hbm,
    dv_hbm,
    gains_hbm,
    order,
    q_gain,
    k_gain,
    gains_out,
    k_in,
    v_in,
    q_buf,
    g_buf,
    q_normed,
    g_cols,
    q_unit,
    q_factor,
    gain_cols,
    own_kv,
    kv,
    kt,
    bias,
    e_all,
    x_all,
    sums,
    stat,
    w_all,
    near_sum,
    own_sum,
    dq_buf,
    gain_acc,
    b1_out,
    b1_in,
    b2_out,
    b2_in,
    sib_out,
    sib_in,
    fin_sum,
    fin_factor,
    fin_unit,
    dk_buf,
    dv_buf,
    ga_in,
    gb_in,
    load_sem,
    qx_send,
    qx_recv,
    s1_send,
    s1_recv,
    s2_send,
    s2_recv,
    sk_send,
    sk_recv,
    b1_send,
    b1_recv,
    b2_send,
    b2_recv,
    sb_send,
    sb_recv,
    out_sem,
    ox_send,
    ox_recv,
    ga_send,
    ga_recv,
    gb_send,
    gb_recv,
    fin_sem,
):
    ctx = lax.axis_index("ctx")
    dp = lax.axis_index("dp")
    chip = ctx // 2
    core = ctx % 2
    other = 1 - core
    sibling = 2 * chip + other
    near = (lax.rem(chip + 1, 4), lax.rem(chip + 3, 4))
    dp_z = dp % 2
    dp_xy = dp // 2
    ring_at = dp_z * 8 + ctx

    def ring_peer(m):
        return {"dp": dp_xy * 2 + m // 8, "ctx": m % 8}

    def plane_peer(m):
        return {"dp": m * 2 + dp_z}

    def remote(src, dst, ssem, rsem, dev):
        return pltpu.make_async_remote_copy(
            src_ref=src, dst_ref=dst, send_sem=ssem, recv_sem=rsem, device_id=dev, device_id_type=MESH
        )

    def head_cols(core_at, u):
        return pl.ds(pl.multiple_of(core_at * 2048 + u * 1024, 1024), 1024)

    barrier = pltpu.get_barrier_semaphore()

    def greet(dev):
        pl.semaphore_signal(barrier, inc=1, device_id=dev, device_id_type=MESH)

    def greet_ring(i, carry):
        greet({"dp": dp_xy * 2 + 1 - dp_z, "ctx": i})
        return carry

    def greet_plane(r, carry):
        greet(plane_peer(lax.rem(dp_xy + r, 16)))
        return carry

    for i in (near[0], near[1], lax.rem(chip + 2, 4)):
        for k in range(2):
            greet({"ctx": 2 * i + k})
    greet({"ctx": sibling})
    loads = [
        pltpu.make_async_copy(k_hbm.at[0], k_in, load_sem.at[0]),
        pltpu.make_async_copy(k_gain_hbm, k_gain, load_sem.at[6]),
        pltpu.make_async_copy(v_hbm.at[0], v_in, load_sem.at[1]),
        pltpu.make_async_copy(q_gain_hbm, q_gain, load_sem.at[7]),
        pltpu.make_async_copy(order_hbm, order, load_sem.at[8]),
    ]
    for c in loads:
        c.start()
    lax.fori_loop(0, 8, greet_ring, 0)
    lax.fori_loop(1, 16, greet_plane, 0)
    load_q = []
    for u in range(2):
        pair = (
            pltpu.make_async_copy(q_hbm.at[0, :, head_cols(core, u)], q_buf.at[u, 0], load_sem.at[2 + 2 * u]),
            pltpu.make_async_copy(g_hbm.at[0, :, head_cols(core, u)], g_buf.at[u, 0], load_sem.at[3 + 2 * u]),
        )
        load_q.append(pair)
        for c in pair:
            c.start()

    for c in loads:
        c.wait()
    k_gain_row = k_gain[...]
    for h in range(HK):
        block = k_in[:, h * HD : (h + 1) * HD].astype(F32)
        factor = lax.rsqrt(jnp.mean(block * block, -1, keepdims=True) + EPS)
        own_kv[h, 0] = (block * factor * k_gain_row).astype(BF)
        own_kv[h, 1] = v_in[:, h * HD : (h + 1) * HD]

    pl.semaphore_wait(barrier, 30)

    lands = (3, 1)

    def stage1(u, d, dest_core, part):
        return remote(
            own_kv.at[2 * dest_core + u, part],
            kv.at[u, part, 2 * lands[d] + core],
            s1_send.at[u, d, dest_core, part],
            s1_recv.at[u, d, core, part],
            {"ctx": 2 * near[d] + dest_core},
        )

    def stage1_arrival(u, d, src_core, part):
        at = kv.at[u, part, 2 * lands[d] + src_core]
        return remote(at, at, s1_send.at[u, d, src_core, part], s1_recv.at[u, d, src_core, part], {"ctx": sibling})

    def sibling_kv(u):
        return remote(own_kv.at[2 * other + u], kv.at[u, :, core], sk_send.at[u], sk_recv.at[u], {"ctx": sibling})

    def sibling_kv_arrival(u):
        return remote(own_kv.at[2 * core + u], kv.at[u, :, other], sk_send.at[u], sk_recv.at[u], {"ctx": sibling})

    def stage2(u, d, src_core):
        return remote(
            kv.at[u, d, 2 * lands[d] + src_core],
            kv.at[u, d, 4 + src_core],
            s2_send.at[u, d, src_core],
            s2_recv.at[u, d, src_core],
            {"ctx": 2 * near[d] + core},
        )

    def stage2_arrival(u, d, src_core):
        at = kv.at[u, d, 4 + src_core]
        return remote(at, at, s2_send.at[u, d, src_core], s2_recv.at[u, d, src_core], {"ctx": sibling})

    def q_exchange(u):
        return (
            remote(q_hbm.at[0, :, head_cols(other, u)], q_buf.at[u, 1], qx_send.at[u, 0], qx_recv.at[u, 0], {"ctx": sibling}),
            remote(g_hbm.at[0, :, head_cols(other, u)], g_buf.at[u, 1], qx_send.at[u, 1], qx_recv.at[u, 1], {"ctx": sibling}),
        )

    by_core = (core, other)

    def share(u):
        sibling_kv(u).start()
        for c in q_exchange(u):
            c.start()

    def gather_start(u):
        for first in range(2):
            for dest_core in by_core:
                for d in range(2):
                    stage1(u, d, dest_core, d if first == 0 else 1 - d).start()

    def forward(u, src_core):
        for d in range(2):
            stage1_arrival(u, d, src_core, d).wait_recv()
            stage2(u, d, src_core).start()

    def near_gather(u):
        for src_core in range(2):
            for d in range(2):
                stage1_arrival(u, d, src_core, 1 - d).wait_recv()
        sibling_kv_arrival(u).wait_recv()

    def far_gather(u):
        for src_core in range(2):
            for d in range(2):
                stage2_arrival(u, d, src_core).wait_recv()

    def prepare_rows(u, rel):
        if rel == 0:
            for c in load_q[u]:
                c.wait()
        else:
            for c in q_exchange(u):
                c.wait_recv()

        def one(hp, carry):
            prepare(u, rel, hp, q_buf, g_buf, q_normed, g_cols, q_unit, q_factor, gain_cols)
            return carry

        lax.fori_loop(0, 4, one, 0)

    def b1(u, d, kk):
        return remote(
            b1_out.at[u, d, kk], b1_in.at[u, d, kk], b1_send.at[u, d, kk], b1_recv.at[u, d, kk], {"ctx": 2 * near[d] + core}
        )

    def b2(u, d, dest_core, part):
        return remote(
            b2_out.at[u, d, dest_core, part],
            b2_in.at[u, d, core, part],
            b2_send.at[u, d, dest_core, part],
            b2_recv.at[u, d, core, part],
            {"ctx": 2 * near[d] + dest_core},
        )

    def b2_arrival(u, d, src_core, part):
        at = b2_in.at[u, d, src_core, part]
        return remote(at, at, b2_send.at[u, d, src_core, part], b2_recv.at[u, d, src_core, part], {"ctx": sibling})

    def sibling_sum(u):
        return remote(sib_out.at[u], sib_in.at[u], sb_send.at[u], sb_recv.at[u], {"ctx": sibling})

    def key_sums(u, slot):
        both = key_part(u, slot, e_all, x_all, w_all)
        k_rows = kv[u, 0, 2 * slot : 2 * slot + 2].reshape(2 * T, HD).astype(F32)
        gain_acc[...] += jnp.sum((both[0] * k_rows).reshape(32, 8, HD), 0)
        return [x.reshape(2, T, HD) for x in both]

    def far_sums(u):
        both = key_sums(u, 2)
        for d in range(2):
            b1_out[u, d] = both[d].astype(BF)

    def far_start(u):
        for kk in range(2):
            for d in range(2):
                b1(u, d, kk).start()

    def near_sums(u, d):
        both = key_sums(u, (1, 3)[d])
        b2_out[u, d, :, 1 - d] = both[1 - d].astype(BF)
        near_sum[u, d] = both[d]

    def near_start(u, d):
        for dest_core in range(2):
            b2(u, d, dest_core, 1 - d).start()

    def own_sums(u):
        both = key_sums(u, 0)
        for part in range(2):
            own_sum[u, part] = both[part]
            sib_out[u, part] = own_sum[u, part, other].astype(BF)
        sibling_sum(u).start()

    def reduce_middle(u, kk):
        for d in range(2):
            b1(u, d, kk).wait_recv()
            b2_out[u, d, kk, d] = (near_sum[u, d, kk] + b1_in[u, d, kk].astype(F32)).astype(BF)
            b2(u, d, kk, d).start()

    def early_finish(u):
        sibling_sum(u).wait_recv()
        for d in range(2):
            for src_core in range(2):
                b2_arrival(u, d, src_core, 1 - d).wait_recv()
        for rel in range(2):
            at = core if rel == 0 else other
            for part in range(2):
                own = own_sum[u, part, core] if rel == 0 else sib_in[u, part].astype(F32)
                fin_sum[rel, part] = own + b2_in[u, 1 - part, at, part].astype(F32)
            block = k_in[:, pl.ds(pl.multiple_of(at * 256 + u * HD, HD), HD)].astype(F32)
            factor = lax.rsqrt(jnp.mean(block * block, -1, keepdims=True) + EPS)
            fin_factor[rel] = jnp.broadcast_to(factor, (T, HD))
            fin_unit[rel] = block * factor

    def late_finish(u):
        for d in range(2):
            for src_core in range(2):
                b2_arrival(u, d, src_core, d).wait_recv()
        for rel in range(2):
            at = core if rel == 0 else other
            cols = pl.ds(pl.multiple_of(at * 256 + u * HD, HD), HD)
            unit = fin_unit[rel]
            scaled = (fin_sum[rel, 0] + b2_in[u, 0, at, 0].astype(F32)) * k_gain_row
            mean = jnp.mean(scaled * unit, -1, keepdims=True)
            dk_buf[:, cols] = (fin_factor[rel] * (scaled - unit * mean)).astype(BF)
            dv_buf[:, cols] = (fin_sum[rel, 1] + b2_in[u, 1, at, 1].astype(F32)).astype(BF)

    def out_local(u):
        return pltpu.make_async_copy(dq_buf.at[u, 0], dq_hbm.at[0, :, head_cols(core, u)], out_sem.at[u])

    def out_remote(u):
        return remote(dq_buf.at[u, 1], dq_hbm.at[0, :, head_cols(core, u)], ox_send.at[u], ox_recv.at[u], {"ctx": sibling})

    def out_arrival(u):
        return remote(dq_buf.at[u, 1], dq_hbm.at[0, :, head_cols(other, u)], ox_send.at[u], ox_recv.at[u], {"ctx": sibling})

    def softmax_parts(u, slots):
        def one(r, carry):
            softmax_part(u, r, slots, kv, q_normed, g_cols, bias, e_all, x_all, sums, stat, w_all)
            return carry

        lax.fori_loop(0, 4, one, 0, unroll=2)

    def query_parts(u):
        kt[u] = kv[u, 0].reshape(KEYS, HD).T

        def one(r, carry):
            query_part(u, r, kt, e_all, x_all, stat, q_unit, q_factor, gain_cols, dq_buf)
            return carry

        lax.fori_loop(0, 2, one, 0)
        out_local(u).start()
        out_remote(u).start()

    gather_start(0)
    share(0)
    share(1)
    for u in range(2):
        for part in range(2):
            kv[u, part, core] = own_kv[2 * core + u, part]
    column = jnp.broadcast_to(q_gain[...], (HD, HD)).T
    gain_cols[...] = jnp.concatenate([column, column], 1)
    gain_acc[...] = jnp.zeros_like(gain_acc)
    make_bias(bias, order, chip, core)
    prepare_rows(0, 0)
    for at in by_core:
        forward(0, at)
    gather_start(1)
    prepare_rows(0, 1)
    prepare_rows(1, 0)
    prepare_rows(1, 1)
    near_gather(0)
    softmax_parts(0, NEAR_SLOTS)
    far_gather(0)
    softmax_parts(0, FAR_SLOTS)
    far_sums(0)
    forward(1, core)
    near_sums(0, 0)
    near_sums(0, 1)
    forward(1, other)
    far_start(0)
    near_start(0, 0)
    near_start(0, 1)
    own_sums(0)
    near_gather(1)
    softmax_parts(1, NEAR_SLOTS)
    far_gather(1)
    softmax_parts(1, FAR_SLOTS)
    reduce_middle(0, 0)
    far_sums(1)
    far_start(1)
    near_sums(1, 0)
    near_start(1, 0)
    reduce_middle(0, 1)
    near_sums(1, 1)
    near_start(1, 1)
    own_sums(1)

    def ga(r):
        return remote(ga_in.at[ring_at], ga_in.at[ring_at], ga_send.at[r], ga_recv.at[ring_at], ring_peer(lax.rem(ring_at + r, 16)))

    def ga_arrival(r):
        j = lax.rem(ring_at + r, 16)
        return remote(ga_in.at[j], ga_in.at[j], ga_send.at[r], ga_recv.at[j], {"ctx": sibling})

    def gb(r):
        return remote(gb_in.at[dp_xy], gb_in.at[dp_xy], gb_send.at[r], gb_recv.at[dp_xy], plane_peer(lax.rem(dp_xy + r, 16)))

    def gb_arrival(r):
        j = lax.rem(dp_xy + r, 16)
        return remote(gb_in.at[j], gb_in.at[j], gb_send.at[r], gb_recv.at[j], {"ctx": sibling})

    def for_peers(act):
        def one(r, carry):
            act(r)
            return carry

        lax.fori_loop(1, 16, one, 0)

    gb_in[dp_xy] = jnp.sum(gain_acc[...], 0, keepdims=True)
    for_peers(lambda r: gb(r).start())
    query_parts(0)
    for_peers(lambda r: gb_arrival(r).wait_recv())
    ga_in[ring_at] = jnp.sum(gb_in[...], 0)
    for_peers(lambda r: ga(r).start())
    reduce_middle(1, 0)
    reduce_middle(1, 1)
    query_parts(1)
    early_finish(0)
    late_finish(0)
    early_finish(1)
    for u in range(2):
        for d in range(2):
            for dest_core in range(2):
                for part in range(2):
                    stage1(u, d, dest_core, part).wait_send()
                stage2(u, d, dest_core).wait_send()
                b1(u, d, dest_core).wait_send()
                b2(u, d, dest_core, 1 - d).wait_send()
                if u == 0:
                    b2(u, d, dest_core, d).wait_send()
        sibling_kv(u).wait_send()
        sibling_sum(u).wait_send()
        for c in q_exchange(u):
            c.wait_send()
        out_local(u).wait()
        out_remote(u).wait_send()
        out_arrival(u).wait_recv()
    for_peers(lambda r: gb(r).wait_send())
    for_peers(lambda r: ga(r).wait_send())
    for_peers(lambda r: ga_arrival(r).wait_recv())
    gain_sum = jnp.sum(ga_in[...], 0)
    gains_out[0:1] = gain_sum / q_gain[...]
    gains_out[1:2] = gain_sum / k_gain_row
    fin_g = pltpu.make_async_copy(gains_out, gains_hbm, fin_sem.at[2])
    fin_g.start()
    late_finish(1)
    fin_k = pltpu.make_async_copy(dk_buf, dk_hbm.at[0], fin_sem.at[0])
    fin_v = pltpu.make_async_copy(dv_buf, dv_hbm.at[0], fin_sem.at[1])
    fin_k.start()
    fin_v.start()
    for d in range(2):
        for dest_core in range(2):
            b2(1, d, dest_core, d).wait_send()
    fin_g.wait()
    fin_k.wait()
    fin_v.wait()


def settle(dq, dk, dv, gains, dq_out, dk_out, dv_out, q_gain_out, k_gain_out, sems):
    pairs = [(gains.at[0], q_gain_out), (gains.at[1], k_gain_out), (dk, dk_out), (dv, dv_out)]
    for i in range(4):
        rows = pl.ds(i * 32, 32)
        pairs.append((dq.at[0, rows], dq_out.at[0, rows]))
    copies = [pltpu.make_async_copy(a, b, sems.at[i]) for i, (a, b) in enumerate(pairs)]
    for c in copies:
        c.start()
    for c in copies:
        c.wait()


def on_device(queries, keys, values, q_gain, k_gain, out_grad, block_order):
    hbm = pl.BlockSpec(memory_space=pl.ANY)
    dma = pltpu.SemaphoreType.DMA
    sends = [dma((2, 2)), dma((2, 2, 2, 2)), dma((2, 2, 2)), dma((2,)), dma((2, 2, 2)), dma((2, 2, 2, 2)), dma((2,))]
    operands = (block_order, queries, keys, values, q_gain.reshape(1, HD), k_gain.reshape(1, HD), out_grad)
    results = pl.pallas_call(
        kernel,
        out_shape=(
            jax.ShapeDtypeStruct(queries.shape, BF),
            jax.ShapeDtypeStruct(keys.shape, BF),
            jax.ShapeDtypeStruct(values.shape, BF),
            jax.ShapeDtypeStruct((2, HD), F32),
        ),
        in_specs=[pl.BlockSpec(memory_space=pltpu.HBM)] * 7,
        out_specs=(hbm,) * 4,
        scratch_shapes=[
            pltpu.SMEM((1, 8), jnp.int32),
            pltpu.VMEM((1, HD), F32),
            pltpu.VMEM((1, HD), F32),
            pltpu.VMEM((2, HD), F32),
            pltpu.VMEM((T, HK * HD), BF),
            pltpu.VMEM((T, HK * HD), BF),
            pltpu.VMEM((2, 2, T, 1024), BF),
            pltpu.VMEM((2, 2, T, 1024), BF),
            pltpu.VMEM((2, HD, ROWS), BF),
            pltpu.VMEM((2, HD, ROWS), BF),
            pltpu.VMEM((2, HD, ROWS), F32),
            pltpu.VMEM((2, 8, ROWS), F32),
            pltpu.VMEM((HD, 256), F32),
            pltpu.VMEM((HK, 2, T, HD), BF),
            pltpu.VMEM((2, 2, 8, T, HD), BF),
            pltpu.VMEM((2, HD, KEYS), BF),
            pltpu.VMEM((2, 8, T, T), F32),
            pltpu.VMEM((2, KEYS, ROWS), BF),
            pltpu.VMEM((2, KEYS, ROWS), BF),
            pltpu.VMEM((2, 8, ROWS), F32),
            pltpu.VMEM((2, 2, 8, ROWS), F32),
            pltpu.VMEM((2, 3 * HD, ROWS), BF),
            pltpu.VMEM((2, 2, 2, T, HD), F32),
            pltpu.VMEM((2, 2, 2, T, HD), F32),
            pltpu.VMEM((2, 2, T, 1024), BF),
            pltpu.VMEM((8, HD), F32),
            pltpu.VMEM((2, 2, 2, T, HD), BF),
            pltpu.VMEM((2, 2, 2, T, HD), BF),
            pltpu.VMEM((2, 2, 2, 2, T, HD), BF),
            pltpu.VMEM((2, 2, 2, 2, T, HD), BF),
            pltpu.VMEM((2, 2, T, HD), BF),
            pltpu.VMEM((2, 2, T, HD), BF),
            pltpu.VMEM((2, 2, T, HD), F32),
            pltpu.VMEM((2, T, HD), F32),
            pltpu.VMEM((2, T, HD), F32),
            pltpu.VMEM((T, HK * HD), BF),
            pltpu.VMEM((T, HK * HD), BF),
            pltpu.VMEM((16, 1, HD), F32),
            pltpu.VMEM((16, 1, HD), F32),
            dma((9,)),
        ]
        + [s for s in sends for _ in range(2)]
        + [dma((2,)), dma((2,)), dma((2,))]
        + [dma((16,)) for _ in range(4)]
        + [dma((3,))],
        compiler_params=pltpu.CompilerParams(
            collective_id=0, has_side_effects=True, vmem_limit_bytes=44 * 1024 * 1024
        ),
    )(*(pltpu.with_memory_space_constraint(x, pltpu.HBM) for x in operands))
    return pl.pallas_call(
        settle,
        out_shape=(
            jax.ShapeDtypeStruct(queries.shape, BF),
            jax.ShapeDtypeStruct(keys.shape, BF),
            jax.ShapeDtypeStruct(values.shape, BF),
            jax.ShapeDtypeStruct((HD,), F32),
            jax.ShapeDtypeStruct((HD,), F32),
        ),
        in_specs=[hbm] * 4,
        out_specs=(hbm,) * 5,
        scratch_shapes=[dma((8,))],
        compiler_params=pltpu.CompilerParams(vmem_limit_bytes=16 * 1024 * 1024),
    )(*results)


def solution(mesh):
    placed = (
        P("dp", "ctx", None),
        P("dp", "ctx", None),
        P("dp", "ctx", None),
        P(),
        P(),
        P("dp", "ctx", None),
        P("dp", None),
    )
    return jax.shard_map(
        on_device,
        mesh=mesh,
        in_specs=placed,
        out_specs=(P("dp", "ctx", None), P("dp", "ctx", None), P("dp", "ctx", None), P(), P()),
        check_vma=False,
    )
```

```python
import math

import jax
import jax.numpy as jnp
from jax import lax
from jax.experimental import pallas as pl
from jax.experimental.pallas import tpu as pltpu
from jax.sharding import PartitionSpec as P

HK = 4
HD = 128
T = 128
KEYS = 8 * T
ROWS = 16 * T
EPS = 1e-06
SCALE = 1.0 / math.sqrt(HD)
EXP2_SCALE = SCALE * math.log2(math.e)
NEG = -1e30
BF = jnp.bfloat16
F32 = jnp.float32
MESH = pl.DeviceIdType.MESH
NT = (((1,), (1,)), ((), ()))
NN = (((1,), (0,)), ((), ()))

NEAR_SLOTS = (0, 1, 3)
FAR_SLOTS = (2,)


def dot(a, b, dims):
    return lax.dot_general(a, b, dims, preferred_element_type=F32)


def make_bias(bias, order, chip, core):
    keys_at = lax.broadcasted_iota(jnp.int32, (T, T), 0)
    rows_at = lax.broadcasted_iota(jnp.int32, (T, T), 1)
    for rel in range(2):
        own = order[0, 2 * chip + (core if rel == 0 else 1 - core)]
        for j in range(8):
            block = order[0, 2 * lax.rem(chip + j // 2, 4) + j % 2]
            bias[rel, j] = jnp.where(block * T + keys_at <= own * T + rows_at, 0.0, NEG)


def prepare(u, rel, hp, q_buf, g_buf, q_normed, g_cols, q_unit, q_factor, gain_cols):
    cols = pl.ds(pl.multiple_of(hp * 256, 256), 256)
    out = pl.ds(pl.multiple_of(rel * 1024 + hp * 256, 256), 256)
    q2 = q_buf[u, rel, :, cols].astype(F32)
    g2 = g_buf[u, rel, :, cols].astype(F32)
    q = jnp.concatenate([q2[:, :HD].T, q2[:, HD:].T], 1)
    factor = lax.rsqrt(jnp.mean(q * q, 0, keepdims=True) + EPS)
    unit = q * factor
    q_factor[u, :, out] = jnp.broadcast_to(factor, (8, 256))
    q_unit[u, :, out] = unit
    q_normed[u, :, out] = (unit * gain_cols[...]).astype(BF)
    g_cols[u, :, out] = jnp.concatenate([g2[:, :HD].T, g2[:, HD:].T], 1).astype(BF)


def softmax_part(u, r, slots, kv, q_normed, g_cols, bias, e_all, x_all, sums, stat, w_all):
    rel = r // 2
    cols = pl.ds(pl.multiple_of(r * 512, 512), 512)
    qn = q_normed[u, :, cols]
    g = g_cols[u, :, cols]
    first = slots == NEAR_SLOTS
    total = jnp.zeros((8, 512), F32) if first else sums[0, :, cols]
    cross = jnp.zeros((8, 512), F32) if first else sums[1, :, cols]
    half = T // 2
    for j in (2 * slot for slot in slots):
        s = dot(kv[u, 0, j : j + 2].reshape(2 * T, HD), qn, NN)
        d = dot(kv[u, 1, j : j + 2].reshape(2 * T, HD), g, NN)
        for b in range(4):
            at, row = b * half, j * T + b * half
            tile = bias[rel, j + b // 2, (b % 2) * half : (b % 2 + 1) * half, :]
            tile = jnp.concatenate([tile] * 4, 1)
            e = jnp.exp2(s[at : at + half] * EXP2_SCALE + tile)
            x = e * d[at : at + half]
            total = total + jnp.sum(e.reshape(half // 8, 8, 512), 0)
            cross = cross + jnp.sum(x.reshape(half // 8, 8, 512), 0)
            e_all[u, row : row + half, cols] = e.astype(BF)
            x_all[u, row : row + half, cols] = x.astype(BF)
    if first:
        sums[0, :, cols] = total
        sums[1, :, cols] = cross
        return
    inv = 1.0 / jnp.sum(total, 0, keepdims=True)
    row_dots = jnp.sum(cross, 0, keepdims=True) * inv
    stat[u, 0, :, cols] = jnp.broadcast_to(inv * SCALE, (8, 512))
    stat[u, 1, :, cols] = jnp.broadcast_to(row_dots, (8, 512))
    scaled = qn.astype(F32) * inv
    w_all[u, 0:128, cols] = (g.astype(F32) * inv).astype(BF)
    w_all[u, 128:256, cols] = (scaled * -row_dots).astype(BF)
    w_all[u, 256:384, cols] = scaled.astype(BF)


def key_part(u, slot, e_all, x_all, w_all):
    at = slice(slot * 256, slot * 256 + 256)
    both = dot(e_all[u, at, :], w_all[u, 0:256, :], NT)
    dk = (both[:, HD:] + dot(x_all[u, at, :], w_all[u, 256:384, :], NT)) * SCALE
    return dk, both[:, :HD]


def query_part(u, r, kt, e_all, x_all, stat, q_unit, q_factor, gain_cols, dq_buf):
    rel = r
    rows = pl.ds(pl.multiple_of(r * 1024, 1024), 1024)
    x = dot(kt[u], x_all[u, :, rows], NN)
    e = dot(kt[u], e_all[u, :, rows], NN)
    dq = (x - e * stat[u, 1, 0:1, rows]) * stat[u, 0, 0:1, rows]
    unit = q_unit[u, :, rows]
    gain = gain_cols[...]
    scaled = dq * jnp.concatenate([gain] * 4, 1)
    mean = jnp.mean(scaled * unit, 0, keepdims=True)
    out = q_factor[u, 0:1, rows] * (scaled - unit * mean)
    dq_buf[u, rel] = jnp.concatenate([out[:, i * HD : i * HD + HD].T for i in range(8)], 1).astype(BF)


def kernel(
    order_hbm,
    q_hbm,
    k_hbm,
    v_hbm,
    q_gain_hbm,
    k_gain_hbm,
    g_hbm,
    dq_hbm,
    dk_hbm,
    dv_hbm,
    gains_hbm,
    order,
    q_gain,
    k_gain,
    gains_out,
    k_in,
    v_in,
    q_buf,
    g_buf,
    q_normed,
    g_cols,
    q_unit,
    q_factor,
    gain_cols,
    own_kv,
    kv,
    kt,
    bias,
    e_all,
    x_all,
    sums,
    stat,
    w_all,
    near_sum,
    own_sum,
    dq_buf,
    gain_acc,
    b1_out,
    b1_in,
    b2_out,
    b2_in,
    sib_out,
    sib_in,
    fin_sum,
    fin_factor,
    fin_unit,
    dk_buf,
    dv_buf,
    ga_in,
    gb_in,
    load_sem,
    qx_send,
    qx_recv,
    s1_send,
    s1_recv,
    s2_send,
    s2_recv,
    sk_send,
    sk_recv,
    b1_send,
    b1_recv,
    b2_send,
    b2_recv,
    sb_send,
    sb_recv,
    out_sem,
    ox_send,
    ox_recv,
    ga_send,
    ga_recv,
    gb_send,
    gb_recv,
    fin_sem,
):
    ctx = lax.axis_index("ctx")
    dp = lax.axis_index("dp")
    chip = ctx // 2
    core = ctx % 2
    other = 1 - core
    sibling = 2 * chip + other
    near = (lax.rem(chip + 1, 4), lax.rem(chip + 3, 4))
    dp_z = dp % 2
    dp_xy = dp // 2
    ring_at = dp_z * 8 + ctx

    def ring_peer(m):
        return {"dp": dp_xy * 2 + m // 8, "ctx": m % 8}

    def plane_peer(m):
        return {"dp": m * 2 + dp_z}

    def remote(src, dst, ssem, rsem, dev):
        return pltpu.make_async_remote_copy(
            src_ref=src, dst_ref=dst, send_sem=ssem, recv_sem=rsem, device_id=dev, device_id_type=MESH
        )

    def head_cols(core_at, u):
        return pl.ds(pl.multiple_of(core_at * 2048 + u * 1024, 1024), 1024)

    barrier = pltpu.get_barrier_semaphore()

    def greet(dev):
        pl.semaphore_signal(barrier, inc=1, device_id=dev, device_id_type=MESH)

    def greet_ring(i, carry):
        greet({"dp": dp_xy * 2 + 1 - dp_z, "ctx": i})
        return carry

    def greet_plane(r, carry):
        greet(plane_peer(lax.rem(dp_xy + r, 16)))
        return carry

    for i in (near[0], near[1], lax.rem(chip + 2, 4)):
        for k in range(2):
            greet({"ctx": 2 * i + k})
    greet({"ctx": sibling})
    loads = [
        pltpu.make_async_copy(k_hbm.at[0], k_in, load_sem.at[0]),
        pltpu.make_async_copy(k_gain_hbm, k_gain, load_sem.at[6]),
        pltpu.make_async_copy(v_hbm.at[0], v_in, load_sem.at[1]),
        pltpu.make_async_copy(q_gain_hbm, q_gain, load_sem.at[7]),
        pltpu.make_async_copy(order_hbm, order, load_sem.at[8]),
    ]
    for c in loads:
        c.start()
    lax.fori_loop(0, 8, greet_ring, 0)
    lax.fori_loop(1, 16, greet_plane, 0)
    load_q = []
    for u in range(2):
        pair = (
            pltpu.make_async_copy(q_hbm.at[0, :, head_cols(core, u)], q_buf.at[u, 0], load_sem.at[2 + 2 * u]),
            pltpu.make_async_copy(g_hbm.at[0, :, head_cols(core, u)], g_buf.at[u, 0], load_sem.at[3 + 2 * u]),
        )
        load_q.append(pair)
        for c in pair:
            c.start()

    for c in loads:
        c.wait()
    k_gain_row = k_gain[...]
    for h in range(HK):
        block = k_in[:, h * HD : (h + 1) * HD].astype(F32)
        factor = lax.rsqrt(jnp.mean(block * block, -1, keepdims=True) + EPS)
        own_kv[h, 0] = (block * factor * k_gain_row).astype(BF)
        own_kv[h, 1] = v_in[:, h * HD : (h + 1) * HD]

    pl.semaphore_wait(barrier, 30)

    lands = (3, 1)

    def stage1(u, d, dest_core, part):
        return remote(
            own_kv.at[2 * dest_core + u, part],
            kv.at[u, part, 2 * lands[d] + core],
            s1_send.at[u, d, dest_core, part],
            s1_recv.at[u, d, core, part],
            {"ctx": 2 * near[d] + dest_core},
        )

    def stage1_arrival(u, d, src_core, part):
        at = kv.at[u, part, 2 * lands[d] + src_core]
        return remote(at, at, s1_send.at[u, d, src_core, part], s1_recv.at[u, d, src_core, part], {"ctx": sibling})

    def sibling_kv(u):
        return remote(own_kv.at[2 * other + u], kv.at[u, :, core], sk_send.at[u], sk_recv.at[u], {"ctx": sibling})

    def sibling_kv_arrival(u):
        return remote(own_kv.at[2 * core + u], kv.at[u, :, other], sk_send.at[u], sk_recv.at[u], {"ctx": sibling})

    def stage2(u, d, src_core):
        return remote(
            kv.at[u, d, 2 * lands[d] + src_core],
            kv.at[u, d, 4 + src_core],
            s2_send.at[u, d, src_core],
            s2_recv.at[u, d, src_core],
            {"ctx": 2 * near[d] + core},
        )

    def stage2_arrival(u, d, src_core):
        at = kv.at[u, d, 4 + src_core]
        return remote(at, at, s2_send.at[u, d, src_core], s2_recv.at[u, d, src_core], {"ctx": sibling})

    def q_exchange(u):
        return (
            remote(q_hbm.at[0, :, head_cols(other, u)], q_buf.at[u, 1], qx_send.at[u, 0], qx_recv.at[u, 0], {"ctx": sibling}),
            remote(g_hbm.at[0, :, head_cols(other, u)], g_buf.at[u, 1], qx_send.at[u, 1], qx_recv.at[u, 1], {"ctx": sibling}),
        )

    by_core = (core, other)

    def share(u):
        sibling_kv(u).start()
        for c in q_exchange(u):
            c.start()

    def gather_start(u):
        for first in range(2):
            for dest_core in by_core:
                for d in range(2):
                    stage1(u, d, dest_core, d if first == 0 else 1 - d).start()

    def forward(u, src_core):
        for d in range(2):
            stage1_arrival(u, d, src_core, d).wait_recv()
            stage2(u, d, src_core).start()

    def near_gather(u):
        for src_core in range(2):
            for d in range(2):
                stage1_arrival(u, d, src_core, 1 - d).wait_recv()
        sibling_kv_arrival(u).wait_recv()

    def far_gather(u):
        for src_core in range(2):
            for d in range(2):
                stage2_arrival(u, d, src_core).wait_recv()

    def prepare_rows(u, rel):
        if rel == 0:
            for c in load_q[u]:
                c.wait()
        else:
            for c in q_exchange(u):
                c.wait_recv()

        def one(hp, carry):
            prepare(u, rel, hp, q_buf, g_buf, q_normed, g_cols, q_unit, q_factor, gain_cols)
            return carry

        lax.fori_loop(0, 4, one, 0)

    def b1(u, d, kk):
        return remote(
            b1_out.at[u, d, kk], b1_in.at[u, d, kk], b1_send.at[u, d, kk], b1_recv.at[u, d, kk], {"ctx": 2 * near[d] + core}
        )

    def b2(u, d, dest_core, part):
        return remote(
            b2_out.at[u, d, dest_core, part],
            b2_in.at[u, d, core, part],
            b2_send.at[u, d, dest_core, part],
            b2_recv.at[u, d, core, part],
            {"ctx": 2 * near[d] + dest_core},
        )

    def b2_arrival(u, d, src_core, part):
        at = b2_in.at[u, d, src_core, part]
        return remote(at, at, b2_send.at[u, d, src_core, part], b2_recv.at[u, d, src_core, part], {"ctx": sibling})

    def sibling_sum(u):
        return remote(sib_out.at[u], sib_in.at[u], sb_send.at[u], sb_recv.at[u], {"ctx": sibling})

    def key_sums(u, slot):
        both = key_part(u, slot, e_all, x_all, w_all)
        k_rows = kv[u, 0, 2 * slot : 2 * slot + 2].reshape(2 * T, HD).astype(F32)
        gain_acc[...] += jnp.sum((both[0] * k_rows).reshape(32, 8, HD), 0)
        return [x.reshape(2, T, HD) for x in both]

    def far_sums(u):
        both = key_sums(u, 2)
        for d in range(2):
            b1_out[u, d] = both[d].astype(BF)

    def far_start(u):
        for kk in range(2):
            for d in range(2):
                b1(u, d, kk).start()

    def near_sums(u, d):
        both = key_sums(u, (1, 3)[d])
        b2_out[u, d, :, 1 - d] = both[1 - d].astype(BF)
        near_sum[u, d] = both[d]

    def near_start(u, d):
        for dest_core in range(2):
            b2(u, d, dest_core, 1 - d).start()

    def own_sums(u):
        both = key_sums(u, 0)
        for part in range(2):
            own_sum[u, part] = both[part]
            sib_out[u, part] = own_sum[u, part, other].astype(BF)
        sibling_sum(u).start()

    def reduce_middle(u, kk):
        for d in range(2):
            b1(u, d, kk).wait_recv()
            b2_out[u, d, kk, d] = (near_sum[u, d, kk] + b1_in[u, d, kk].astype(F32)).astype(BF)
            b2(u, d, kk, d).start()

    def early_finish(u):
        sibling_sum(u).wait_recv()
        for d in range(2):
            for src_core in range(2):
                b2_arrival(u, d, src_core, 1 - d).wait_recv()
        for rel in range(2):
            at = core if rel == 0 else other
            for part in range(2):
                own = own_sum[u, part, core] if rel == 0 else sib_in[u, part].astype(F32)
                fin_sum[rel, part] = own + b2_in[u, 1 - part, at, part].astype(F32)
            block = k_in[:, pl.ds(pl.multiple_of(at * 256 + u * HD, HD), HD)].astype(F32)
            factor = lax.rsqrt(jnp.mean(block * block, -1, keepdims=True) + EPS)
            fin_factor[rel] = jnp.broadcast_to(factor, (T, HD))
            fin_unit[rel] = block * factor

    def late_finish(u):
        for d in range(2):
            for src_core in range(2):
                b2_arrival(u, d, src_core, d).wait_recv()
        for rel in range(2):
            at = core if rel == 0 else other
            cols = pl.ds(pl.multiple_of(at * 256 + u * HD, HD), HD)
            unit = fin_unit[rel]
            scaled = (fin_sum[rel, 0] + b2_in[u, 0, at, 0].astype(F32)) * k_gain_row
            mean = jnp.mean(scaled * unit, -1, keepdims=True)
            dk_buf[:, cols] = (fin_factor[rel] * (scaled - unit * mean)).astype(BF)
            dv_buf[:, cols] = (fin_sum[rel, 1] + b2_in[u, 1, at, 1].astype(F32)).astype(BF)

    def out_local(u):
        return pltpu.make_async_copy(dq_buf.at[u, 0], dq_hbm.at[0, :, head_cols(core, u)], out_sem.at[u])

    def out_remote(u):
        return remote(dq_buf.at[u, 1], dq_hbm.at[0, :, head_cols(core, u)], ox_send.at[u], ox_recv.at[u], {"ctx": sibling})

    def out_arrival(u):
        return remote(dq_buf.at[u, 1], dq_hbm.at[0, :, head_cols(other, u)], ox_send.at[u], ox_recv.at[u], {"ctx": sibling})

    def softmax_parts(u, slots):
        def one(r, carry):
            softmax_part(u, r, slots, kv, q_normed, g_cols, bias, e_all, x_all, sums, stat, w_all)
            return carry

        lax.fori_loop(0, 4, one, 0, unroll=2)

    def query_parts(u):
        kt[u] = kv[u, 0].reshape(KEYS, HD).T

        def one(r, carry):
            query_part(u, r, kt, e_all, x_all, stat, q_unit, q_factor, gain_cols, dq_buf)
            return carry

        lax.fori_loop(0, 2, one, 0)
        out_local(u).start()
        out_remote(u).start()

    gather_start(0)
    share(0)
    share(1)
    for u in range(2):
        for part in range(2):
            kv[u, part, core] = own_kv[2 * core + u, part]
    column = jnp.broadcast_to(q_gain[...], (HD, HD)).T
    gain_cols[...] = jnp.concatenate([column, column], 1)
    gain_acc[...] = jnp.zeros_like(gain_acc)
    make_bias(bias, order, chip, core)
    prepare_rows(0, 0)
    for at in by_core:
        forward(0, at)
    gather_start(1)
    prepare_rows(0, 1)
    prepare_rows(1, 0)
    prepare_rows(1, 1)
    near_gather(0)
    softmax_parts(0, NEAR_SLOTS)
    far_gather(0)
    softmax_parts(0, FAR_SLOTS)
    far_sums(0)
    forward(1, core)
    near_sums(0, 0)
    near_sums(0, 1)
    forward(1, other)
    far_start(0)
    near_start(0, 0)
    near_start(0, 1)
    own_sums(0)
    near_gather(1)
    softmax_parts(1, NEAR_SLOTS)
    far_gather(1)
    softmax_parts(1, FAR_SLOTS)
    reduce_middle(0, 0)
    far_sums(1)
    far_start(1)
    near_sums(1, 0)
    near_start(1, 0)
    reduce_middle(0, 1)
    near_sums(1, 1)
    near_start(1, 1)
    own_sums(1)

    def ga(r):
        return remote(ga_in.at[ring_at], ga_in.at[ring_at], ga_send.at[r], ga_recv.at[ring_at], ring_peer(lax.rem(ring_at + r, 16)))

    def ga_arrival(r):
        j = lax.rem(ring_at + r, 16)
        return remote(ga_in.at[j], ga_in.at[j], ga_send.at[r], ga_recv.at[j], {"ctx": sibling})

    def gb(r):
        return remote(gb_in.at[dp_xy], gb_in.at[dp_xy], gb_send.at[r], gb_recv.at[dp_xy], plane_peer(lax.rem(dp_xy + r, 16)))

    def gb_arrival(r):
        j = lax.rem(dp_xy + r, 16)
        return remote(gb_in.at[j], gb_in.at[j], gb_send.at[r], gb_recv.at[j], {"ctx": sibling})

    def for_peers(act):
        def one(r, carry):
            act(r)
            return carry

        lax.fori_loop(1, 16, one, 0)

    gb_in[dp_xy] = jnp.sum(gain_acc[...], 0, keepdims=True)
    for_peers(lambda r: gb(r).start())
    query_parts(0)
    query_parts(1)
    for_peers(lambda r: gb_arrival(r).wait_recv())
    ga_in[ring_at] = jnp.sum(gb_in[...], 0)
    for_peers(lambda r: ga(r).start())
    reduce_middle(1, 0)
    reduce_middle(1, 1)
    early_finish(0)
    late_finish(0)
    early_finish(1)
    for u in range(2):
        for d in range(2):
            for dest_core in range(2):
                for part in range(2):
                    stage1(u, d, dest_core, part).wait_send()
                stage2(u, d, dest_core).wait_send()
                b1(u, d, dest_core).wait_send()
                b2(u, d, dest_core, 1 - d).wait_send()
                if u == 0:
                    b2(u, d, dest_core, d).wait_send()
        sibling_kv(u).wait_send()
        sibling_sum(u).wait_send()
        for c in q_exchange(u):
            c.wait_send()
        out_local(u).wait()
        out_remote(u).wait_send()
        out_arrival(u).wait_recv()
    for_peers(lambda r: gb(r).wait_send())
    for_peers(lambda r: ga(r).wait_send())
    for_peers(lambda r: ga_arrival(r).wait_recv())
    gain_sum = jnp.sum(ga_in[...], 0)
    gains_out[0:1] = gain_sum / q_gain[...]
    gains_out[1:2] = gain_sum / k_gain_row
    fin_g = pltpu.make_async_copy(gains_out, gains_hbm, fin_sem.at[2])
    fin_g.start()
    late_finish(1)
    fin_k = pltpu.make_async_copy(dk_buf, dk_hbm.at[0], fin_sem.at[0])
    fin_v = pltpu.make_async_copy(dv_buf, dv_hbm.at[0], fin_sem.at[1])
    fin_k.start()
    fin_v.start()
    for d in range(2):
        for dest_core in range(2):
            b2(1, d, dest_core, d).wait_send()
    fin_g.wait()
    fin_k.wait()
    fin_v.wait()


def settle(dq, dk, dv, gains, dq_out, dk_out, dv_out, q_gain_out, k_gain_out, sems):
    pairs = [(gains.at[0], q_gain_out), (gains.at[1], k_gain_out), (dk, dk_out), (dv, dv_out)]
    for i in range(4):
        rows = pl.ds(i * 32, 32)
        pairs.append((dq.at[0, rows], dq_out.at[0, rows]))
    copies = [pltpu.make_async_copy(a, b, sems.at[i]) for i, (a, b) in enumerate(pairs)]
    for c in copies:
        c.start()
    for c in copies:
        c.wait()


def on_device(queries, keys, values, q_gain, k_gain, out_grad, block_order):
    hbm = pl.BlockSpec(memory_space=pl.ANY)
    dma = pltpu.SemaphoreType.DMA
    sends = [dma((2, 2)), dma((2, 2, 2, 2)), dma((2, 2, 2)), dma((2,)), dma((2, 2, 2)), dma((2, 2, 2, 2)), dma((2,))]
    operands = (block_order, queries, keys, values, q_gain.reshape(1, HD), k_gain.reshape(1, HD), out_grad)
    results = pl.pallas_call(
        kernel,
        out_shape=(
            jax.ShapeDtypeStruct(queries.shape, BF),
            jax.ShapeDtypeStruct(keys.shape, BF),
            jax.ShapeDtypeStruct(values.shape, BF),
            jax.ShapeDtypeStruct((2, HD), F32),
        ),
        in_specs=[pl.BlockSpec(memory_space=pltpu.HBM)] * 7,
        out_specs=(hbm,) * 4,
        scratch_shapes=[
            pltpu.SMEM((1, 8), jnp.int32),
            pltpu.VMEM((1, HD), F32),
            pltpu.VMEM((1, HD), F32),
            pltpu.VMEM((2, HD), F32),
            pltpu.VMEM((T, HK * HD), BF),
            pltpu.VMEM((T, HK * HD), BF),
            pltpu.VMEM((2, 2, T, 1024), BF),
            pltpu.VMEM((2, 2, T, 1024), BF),
            pltpu.VMEM((2, HD, ROWS), BF),
            pltpu.VMEM((2, HD, ROWS), BF),
            pltpu.VMEM((2, HD, ROWS), F32),
            pltpu.VMEM((2, 8, ROWS), F32),
            pltpu.VMEM((HD, 256), F32),
            pltpu.VMEM((HK, 2, T, HD), BF),
            pltpu.VMEM((2, 2, 8, T, HD), BF),
            pltpu.VMEM((2, HD, KEYS), BF),
            pltpu.VMEM((2, 8, T, T), F32),
            pltpu.VMEM((2, KEYS, ROWS), BF),
            pltpu.VMEM((2, KEYS, ROWS), BF),
            pltpu.VMEM((2, 8, ROWS), F32),
            pltpu.VMEM((2, 2, 8, ROWS), F32),
            pltpu.VMEM((2, 3 * HD, ROWS), BF),
            pltpu.VMEM((2, 2, 2, T, HD), F32),
            pltpu.VMEM((2, 2, 2, T, HD), F32),
            pltpu.VMEM((2, 2, T, 1024), BF),
            pltpu.VMEM((8, HD), F32),
            pltpu.VMEM((2, 2, 2, T, HD), BF),
            pltpu.VMEM((2, 2, 2, T, HD), BF),
            pltpu.VMEM((2, 2, 2, 2, T, HD), BF),
            pltpu.VMEM((2, 2, 2, 2, T, HD), BF),
            pltpu.VMEM((2, 2, T, HD), BF),
            pltpu.VMEM((2, 2, T, HD), BF),
            pltpu.VMEM((2, 2, T, HD), F32),
            pltpu.VMEM((2, T, HD), F32),
            pltpu.VMEM((2, T, HD), F32),
            pltpu.VMEM((T, HK * HD), BF),
            pltpu.VMEM((T, HK * HD), BF),
            pltpu.VMEM((16, 1, HD), F32),
            pltpu.VMEM((16, 1, HD), F32),
            dma((9,)),
        ]
        + [s for s in sends for _ in range(2)]
        + [dma((2,)), dma((2,)), dma((2,))]
        + [dma((16,)) for _ in range(4)]
        + [dma((3,))],
        compiler_params=pltpu.CompilerParams(
            collective_id=0, has_side_effects=True, vmem_limit_bytes=44 * 1024 * 1024
        ),
    )(*(pltpu.with_memory_space_constraint(x, pltpu.HBM) for x in operands))
    return pl.pallas_call(
        settle,
        out_shape=(
            jax.ShapeDtypeStruct(queries.shape, BF),
            jax.ShapeDtypeStruct(keys.shape, BF),
            jax.ShapeDtypeStruct(values.shape, BF),
            jax.ShapeDtypeStruct((HD,), F32),
            jax.ShapeDtypeStruct((HD,), F32),
        ),
        in_specs=[hbm] * 4,
        out_specs=(hbm,) * 5,
        scratch_shapes=[dma((8,))],
        compiler_params=pltpu.CompilerParams(vmem_limit_bytes=16 * 1024 * 1024),
    )(*results)


def solution(mesh):
    placed = (
        P("dp", "ctx", None),
        P("dp", "ctx", None),
        P("dp", "ctx", None),
        P(),
        P(),
        P("dp", "ctx", None),
        P("dp", None),
    )
    return jax.shard_map(
        on_device,
        mesh=mesh,
        in_specs=placed,
        out_specs=(P("dp", "ctx", None), P("dp", "ctx", None), P("dp", "ctx", None), P(), P()),
        check_vma=False,
    )
```

```python
import math

import jax
import jax.numpy as jnp
from jax import lax
from jax.experimental import pallas as pl
from jax.experimental.pallas import tpu as pltpu
from jax.sharding import PartitionSpec as P

HK = 4
HD = 128
T = 128
KEYS = 8 * T
ROWS = 16 * T
EPS = 1e-06
SCALE = 1.0 / math.sqrt(HD)
EXP2_SCALE = SCALE * math.log2(math.e)
NEG = -1e30
BF = jnp.bfloat16
F32 = jnp.float32
MESH = pl.DeviceIdType.MESH
NT = (((1,), (1,)), ((), ()))
NN = (((1,), (0,)), ((), ()))

NEAR_SLOTS = (0, 1, 3)
FAR_SLOTS = (2,)


def dot(a, b, dims):
    return lax.dot_general(a, b, dims, preferred_element_type=F32)


def make_bias(bias, order, chip, core):
    keys_at = lax.broadcasted_iota(jnp.int32, (T, T), 0)
    rows_at = lax.broadcasted_iota(jnp.int32, (T, T), 1)
    for rel in range(2):
        own = order[0, 2 * chip + (core if rel == 0 else 1 - core)]
        for j in range(8):
            block = order[0, 2 * lax.rem(chip + j // 2, 4) + j % 2]
            bias[rel, j] = jnp.where(block * T + keys_at <= own * T + rows_at, 0.0, NEG)


def prepare(u, rel, hp, q_buf, g_buf, q_normed, g_cols, q_unit, q_factor, gain_cols):
    cols = pl.ds(pl.multiple_of(hp * 256, 256), 256)
    out = pl.ds(pl.multiple_of(rel * 1024 + hp * 256, 256), 256)
    q2 = q_buf[u, rel, :, cols].astype(F32)
    g2 = g_buf[u, rel, :, cols].astype(F32)
    q = jnp.concatenate([q2[:, :HD].T, q2[:, HD:].T], 1)
    factor = lax.rsqrt(jnp.mean(q * q, 0, keepdims=True) + EPS)
    unit = q * factor
    q_factor[u, :, out] = jnp.broadcast_to(factor, (8, 256))
    q_unit[u, :, out] = unit
    q_normed[u, :, out] = (unit * gain_cols[...]).astype(BF)
    g_cols[u, :, out] = jnp.concatenate([g2[:, :HD].T, g2[:, HD:].T], 1).astype(BF)


def softmax_part(u, r, slots, kv, q_normed, g_cols, bias, e_all, x_all, sums, stat, w_all):
    rel = r // 4
    cols = pl.ds(pl.multiple_of(r * 256, 256), 256)
    qn = q_normed[u, :, cols]
    g = g_cols[u, :, cols]
    first = slots == NEAR_SLOTS
    total = jnp.zeros((8, 256), F32) if first else sums[0, :, cols]
    cross = jnp.zeros((8, 256), F32) if first else sums[1, :, cols]
    half = T // 2
    for j in (2 * slot for slot in slots):
        s = dot(kv[u, 0, j : j + 2].reshape(2 * T, HD), qn, NN)
        d = dot(kv[u, 1, j : j + 2].reshape(2 * T, HD), g, NN)
        for b in range(4):
            at, row = b * half, j * T + b * half
            tile = bias[rel, j + b // 2, (b % 2) * half : (b % 2 + 1) * half, :]
            tile = jnp.concatenate([tile, tile], 1)
            e = jnp.exp2(s[at : at + half] * EXP2_SCALE + tile)
            x = e * d[at : at + half]
            total = total + jnp.sum(e.reshape(half // 8, 8, 256), 0)
            cross = cross + jnp.sum(x.reshape(half // 8, 8, 256), 0)
            e_all[u, row : row + half, cols] = e.astype(BF)
            x_all[u, row : row + half, cols] = x.astype(BF)
    if first:
        sums[0, :, cols] = total
        sums[1, :, cols] = cross
        return
    inv = 1.0 / jnp.sum(total, 0, keepdims=True)
    row_dots = jnp.sum(cross, 0, keepdims=True) * inv
    stat[u, 0, :, cols] = jnp.broadcast_to(inv * SCALE, (8, 256))
    stat[u, 1, :, cols] = jnp.broadcast_to(row_dots, (8, 256))
    scaled = qn.astype(F32) * inv
    w_all[u, 0:128, cols] = (g.astype(F32) * inv).astype(BF)
    w_all[u, 128:256, cols] = (scaled * -row_dots).astype(BF)
    w_all[u, 256:384, cols] = scaled.astype(BF)


def key_part(u, slot, e_all, x_all, w_all):
    at = slice(slot * 256, slot * 256 + 256)
    both = dot(e_all[u, at, :], w_all[u, 0:256, :], NT)
    dk = (both[:, HD:] + dot(x_all[u, at, :], w_all[u, 256:384, :], NT)) * SCALE
    return dk, both[:, :HD]


def query_part(u, r, kt, e_all, x_all, stat, q_unit, q_factor, gain_cols, dq_buf):
    rel = r
    rows = pl.ds(pl.multiple_of(r * 1024, 1024), 1024)
    x = dot(kt[u], x_all[u, :, rows], NN)
    e = dot(kt[u], e_all[u, :, rows], NN)
    dq = (x - e * stat[u, 1, 0:1, rows]) * stat[u, 0, 0:1, rows]
    unit = q_unit[u, :, rows]
    gain = gain_cols[...]
    scaled = dq * jnp.concatenate([gain] * 4, 1)
    mean = jnp.mean(scaled * unit, 0, keepdims=True)
    out = q_factor[u, 0:1, rows] * (scaled - unit * mean)
    dq_buf[u, rel] = jnp.concatenate([out[:, i * HD : i * HD + HD].T for i in range(8)], 1).astype(BF)


def kernel(
    order_hbm,
    q_hbm,
    k_hbm,
    v_hbm,
    q_gain_hbm,
    k_gain_hbm,
    g_hbm,
    dq_hbm,
    dk_hbm,
    dv_hbm,
    gains_hbm,
    order,
    q_gain,
    k_gain,
    gains_out,
    k_in,
    v_in,
    q_buf,
    g_buf,
    q_normed,
    g_cols,
    q_unit,
    q_factor,
    gain_cols,
    own_kv,
    kv,
    kt,
    bias,
    e_all,
    x_all,
    sums,
    stat,
    w_all,
    near_sum,
    own_sum,
    dq_buf,
    gain_acc,
    b1_out,
    b1_in,
    b2_out,
    b2_in,
    sib_out,
    sib_in,
    fin_sum,
    fin_factor,
    fin_unit,
    dk_buf,
    dv_buf,
    ga_in,
    gb_in,
    load_sem,
    qx_send,
    qx_recv,
    s1_send,
    s1_recv,
    s2_send,
    s2_recv,
    sk_send,
    sk_recv,
    b1_send,
    b1_recv,
    b2_send,
    b2_recv,
    sb_send,
    sb_recv,
    out_sem,
    ox_send,
    ox_recv,
    ga_send,
    ga_recv,
    gb_send,
    gb_recv,
    fin_sem,
):
    ctx = lax.axis_index("ctx")
    dp = lax.axis_index("dp")
    chip = ctx // 2
    core = ctx % 2
    other = 1 - core
    sibling = 2 * chip + other
    near = (lax.rem(chip + 1, 4), lax.rem(chip + 3, 4))
    dp_z = dp % 2
    dp_xy = dp // 2
    ring_at = dp_z * 8 + ctx

    def ring_peer(m):
        return {"dp": dp_xy * 2 + m // 8, "ctx": m % 8}

    def plane_peer(m):
        return {"dp": m * 2 + dp_z}

    def remote(src, dst, ssem, rsem, dev):
        return pltpu.make_async_remote_copy(
            src_ref=src, dst_ref=dst, send_sem=ssem, recv_sem=rsem, device_id=dev, device_id_type=MESH
        )

    def head_cols(core_at, u):
        return pl.ds(pl.multiple_of(core_at * 2048 + u * 1024, 1024), 1024)

    barrier = pltpu.get_barrier_semaphore()

    def greet(dev):
        pl.semaphore_signal(barrier, inc=1, device_id=dev, device_id_type=MESH)

    def greet_ring(i, carry):
        greet({"dp": dp_xy * 2 + 1 - dp_z, "ctx": i})
        return carry

    def greet_plane(r, carry):
        greet(plane_peer(lax.rem(dp_xy + r, 16)))
        return carry

    for i in (near[0], near[1], lax.rem(chip + 2, 4)):
        for k in range(2):
            greet({"ctx": 2 * i + k})
    greet({"ctx": sibling})
    loads = [
        pltpu.make_async_copy(k_hbm.at[0], k_in, load_sem.at[0]),
        pltpu.make_async_copy(k_gain_hbm, k_gain, load_sem.at[6]),
        pltpu.make_async_copy(v_hbm.at[0], v_in, load_sem.at[1]),
        pltpu.make_async_copy(q_gain_hbm, q_gain, load_sem.at[7]),
        pltpu.make_async_copy(order_hbm, order, load_sem.at[8]),
    ]
    for c in loads:
        c.start()
    lax.fori_loop(0, 8, greet_ring, 0)
    lax.fori_loop(1, 16, greet_plane, 0)
    load_q = []
    for u in range(2):
        pair = (
            pltpu.make_async_copy(q_hbm.at[0, :, head_cols(core, u)], q_buf.at[u, 0], load_sem.at[2 + 2 * u]),
            pltpu.make_async_copy(g_hbm.at[0, :, head_cols(core, u)], g_buf.at[u, 0], load_sem.at[3 + 2 * u]),
        )
        load_q.append(pair)
        for c in pair:
            c.start()

    for c in loads:
        c.wait()
    k_gain_row = k_gain[...]
    for h in range(HK):
        block = k_in[:, h * HD : (h + 1) * HD].astype(F32)
        factor = lax.rsqrt(jnp.mean(block * block, -1, keepdims=True) + EPS)
        own_kv[h, 0] = (block * factor * k_gain_row).astype(BF)
        own_kv[h, 1] = v_in[:, h * HD : (h + 1) * HD]

    pl.semaphore_wait(barrier, 30)

    lands = (3, 1)

    def stage1(u, d, dest_core, part):
        return remote(
            own_kv.at[2 * dest_core + u, part],
            kv.at[u, part, 2 * lands[d] + core],
            s1_send.at[u, d, dest_core, part],
            s1_recv.at[u, d, core, part],
            {"ctx": 2 * near[d] + dest_core},
        )

    def stage1_arrival(u, d, src_core, part):
        at = kv.at[u, part, 2 * lands[d] + src_core]
        return remote(at, at, s1_send.at[u, d, src_core, part], s1_recv.at[u, d, src_core, part], {"ctx": sibling})

    def sibling_kv(u):
        return remote(own_kv.at[2 * other + u], kv.at[u, :, core], sk_send.at[u], sk_recv.at[u], {"ctx": sibling})

    def sibling_kv_arrival(u):
        return remote(own_kv.at[2 * core + u], kv.at[u, :, other], sk_send.at[u], sk_recv.at[u], {"ctx": sibling})

    def stage2(u, d, src_core):
        return remote(
            kv.at[u, d, 2 * lands[d] + src_core],
            kv.at[u, d, 4 + src_core],
            s2_send.at[u, d, src_core],
            s2_recv.at[u, d, src_core],
            {"ctx": 2 * near[d] + core},
        )

    def stage2_arrival(u, d, src_core):
        at = kv.at[u, d, 4 + src_core]
        return remote(at, at, s2_send.at[u, d, src_core], s2_recv.at[u, d, src_core], {"ctx": sibling})

    def q_exchange(u):
        return (
            remote(q_hbm.at[0, :, head_cols(other, u)], q_buf.at[u, 1], qx_send.at[u, 0], qx_recv.at[u, 0], {"ctx": sibling}),
            remote(g_hbm.at[0, :, head_cols(other, u)], g_buf.at[u, 1], qx_send.at[u, 1], qx_recv.at[u, 1], {"ctx": sibling}),
        )

    by_core = (core, other)

    def share(u):
        sibling_kv(u).start()
        for c in q_exchange(u):
            c.start()

    def gather_start(u):
        for first in range(2):
            for dest_core in by_core:
                for d in range(2):
                    stage1(u, d, dest_core, d if first == 0 else 1 - d).start()

    def forward(u, src_core):
        for d in range(2):
            stage1_arrival(u, d, src_core, d).wait_recv()
            stage2(u, d, src_core).start()

    def near_gather(u):
        for src_core in range(2):
            for d in range(2):
                stage1_arrival(u, d, src_core, 1 - d).wait_recv()
        sibling_kv_arrival(u).wait_recv()

    def far_gather(u):
        for src_core in range(2):
            for d in range(2):
                stage2_arrival(u, d, src_core).wait_recv()

    def prepare_rows(u, rel):
        if rel == 0:
            for c in load_q[u]:
                c.wait()
        else:
            for c in q_exchange(u):
                c.wait_recv()

        def one(hp, carry):
            prepare(u, rel, hp, q_buf, g_buf, q_normed, g_cols, q_unit, q_factor, gain_cols)
            return carry

        lax.fori_loop(0, 4, one, 0)

    def b1(u, d, kk):
        return remote(
            b1_out.at[u, d, kk], b1_in.at[u, d, kk], b1_send.at[u, d, kk], b1_recv.at[u, d, kk], {"ctx": 2 * near[d] + core}
        )

    def b2(u, d, dest_core, part):
        return remote(
            b2_out.at[u, d, dest_core, part],
            b2_in.at[u, d, core, part],
            b2_send.at[u, d, dest_core, part],
            b2_recv.at[u, d, core, part],
            {"ctx": 2 * near[d] + dest_core},
        )

    def b2_arrival(u, d, src_core, part):
        at = b2_in.at[u, d, src_core, part]
        return remote(at, at, b2_send.at[u, d, src_core, part], b2_recv.at[u, d, src_core, part], {"ctx": sibling})

    def sibling_sum(u):
        return remote(sib_out.at[u], sib_in.at[u], sb_send.at[u], sb_recv.at[u], {"ctx": sibling})

    def key_sums(u, slot):
        both = key_part(u, slot, e_all, x_all, w_all)
        k_rows = kv[u, 0, 2 * slot : 2 * slot + 2].reshape(2 * T, HD).astype(F32)
        gain_acc[...] += jnp.sum((both[0] * k_rows).reshape(32, 8, HD), 0)
        return [x.reshape(2, T, HD) for x in both]

    def far_sums(u):
        both = key_sums(u, 2)
        for d in range(2):
            b1_out[u, d] = both[d].astype(BF)

    def far_start(u):
        for kk in range(2):
            for d in range(2):
                b1(u, d, kk).start()

    def near_sums(u, d):
        both = key_sums(u, (1, 3)[d])
        b2_out[u, d, :, 1 - d] = both[1 - d].astype(BF)
        near_sum[u, d] = both[d]

    def near_start(u, d):
        for dest_core in range(2):
            b2(u, d, dest_core, 1 - d).start()

    def own_sums(u):
        both = key_sums(u, 0)
        for part in range(2):
            own_sum[u, part] = both[part]
            sib_out[u, part] = own_sum[u, part, other].astype(BF)
        sibling_sum(u).start()

    def reduce_middle(u, kk):
        for d in range(2):
            b1(u, d, kk).wait_recv()
            b2_out[u, d, kk, d] = (near_sum[u, d, kk] + b1_in[u, d, kk].astype(F32)).astype(BF)
            b2(u, d, kk, d).start()

    def early_finish(u):
        sibling_sum(u).wait_recv()
        for d in range(2):
            for src_core in range(2):
                b2_arrival(u, d, src_core, 1 - d).wait_recv()
        for rel in range(2):
            at = core if rel == 0 else other
            for part in range(2):
                own = own_sum[u, part, core] if rel == 0 else sib_in[u, part].astype(F32)
                fin_sum[rel, part] = own + b2_in[u, 1 - part, at, part].astype(F32)
            block = k_in[:, pl.ds(pl.multiple_of(at * 256 + u * HD, HD), HD)].astype(F32)
            factor = lax.rsqrt(jnp.mean(block * block, -1, keepdims=True) + EPS)
            fin_factor[rel] = jnp.broadcast_to(factor, (T, HD))
            fin_unit[rel] = block * factor

    def late_finish(u, part):
        for src_core in range(2):
            b2_arrival(u, part, src_core, part).wait_recv()
        for rel in range(2):
            at = core if rel == 0 else other
            cols = pl.ds(pl.multiple_of(at * 256 + u * HD, HD), HD)
            full = fin_sum[rel, part] + b2_in[u, part, at, part].astype(F32)
            if part == 1:
                dv_buf[:, cols] = full.astype(BF)
                continue
            unit = fin_unit[rel]
            scaled = full * k_gain_row
            mean = jnp.mean(scaled * unit, -1, keepdims=True)
            dk_buf[:, cols] = (fin_factor[rel] * (scaled - unit * mean)).astype(BF)

    def out_local(u):
        return pltpu.make_async_copy(dq_buf.at[u, 0], dq_hbm.at[0, :, head_cols(core, u)], out_sem.at[u])

    def out_remote(u):
        return remote(dq_buf.at[u, 1], dq_hbm.at[0, :, head_cols(core, u)], ox_send.at[u], ox_recv.at[u], {"ctx": sibling})

    def out_arrival(u):
        return remote(dq_buf.at[u, 1], dq_hbm.at[0, :, head_cols(other, u)], ox_send.at[u], ox_recv.at[u], {"ctx": sibling})

    def softmax_parts(u, slots):
        def one(r, carry):
            softmax_part(u, r, slots, kv, q_normed, g_cols, bias, e_all, x_all, sums, stat, w_all)
            return carry

        lax.fori_loop(0, 8, one, 0)

    def query_parts(u):
        kt[u] = kv[u, 0].reshape(KEYS, HD).T

        def one(r, carry):
            query_part(u, r, kt, e_all, x_all, stat, q_unit, q_factor, gain_cols, dq_buf)
            return carry

        lax.fori_loop(0, 2, one, 0)
        out_local(u).start()
        out_remote(u).start()

    gather_start(0)
    share(0)
    share(1)
    for u in range(2):
        for part in range(2):
            kv[u, part, core] = own_kv[2 * core + u, part]
    column = jnp.broadcast_to(q_gain[...], (HD, HD)).T
    gain_cols[...] = jnp.concatenate([column, column], 1)
    gain_acc[...] = jnp.zeros_like(gain_acc)
    make_bias(bias, order, chip, core)
    prepare_rows(0, 0)
    for at in by_core:
        forward(0, at)
    gather_start(1)
    prepare_rows(0, 1)
    prepare_rows(1, 0)
    prepare_rows(1, 1)
    near_gather(0)
    softmax_parts(0, NEAR_SLOTS)
    far_gather(0)
    softmax_parts(0, FAR_SLOTS)
    far_sums(0)
    forward(1, core)
    near_sums(0, 0)
    near_sums(0, 1)
    forward(1, other)
    far_start(0)
    near_start(0, 0)
    near_start(0, 1)
    own_sums(0)
    near_gather(1)
    softmax_parts(1, NEAR_SLOTS)
    far_gather(1)
    softmax_parts(1, FAR_SLOTS)
    reduce_middle(0, 0)
    far_sums(1)
    far_start(1)
    near_sums(1, 0)
    near_start(1, 0)
    reduce_middle(0, 1)
    near_sums(1, 1)
    near_start(1, 1)
    own_sums(1)

    def ga(r):
        return remote(ga_in.at[ring_at], ga_in.at[ring_at], ga_send.at[r], ga_recv.at[ring_at], ring_peer(lax.rem(ring_at + r, 16)))

    def ga_arrival(r):
        j = lax.rem(ring_at + r, 16)
        return remote(ga_in.at[j], ga_in.at[j], ga_send.at[r], ga_recv.at[j], {"ctx": sibling})

    def gb(r):
        return remote(gb_in.at[dp_xy], gb_in.at[dp_xy], gb_send.at[r], gb_recv.at[dp_xy], plane_peer(lax.rem(dp_xy + r, 16)))

    def gb_arrival(r):
        j = lax.rem(dp_xy + r, 16)
        return remote(gb_in.at[j], gb_in.at[j], gb_send.at[r], gb_recv.at[j], {"ctx": sibling})

    def for_peers(act):
        def one(r, carry):
            act(r)
            return carry

        lax.fori_loop(1, 16, one, 0)

    gb_in[dp_xy] = jnp.sum(gain_acc[...], 0, keepdims=True)
    for_peers(lambda r: gb(r).start())
    query_parts(0)
    query_parts(1)
    for_peers(lambda r: gb_arrival(r).wait_recv())
    ga_in[ring_at] = jnp.sum(gb_in[...], 0)
    for_peers(lambda r: ga(r).start())
    for kk in range(2):
        reduce_middle(1, kk)
    early_finish(0)
    late_finish(0, 1)
    late_finish(0, 0)
    early_finish(1)
    for u in range(2):
        for d in range(2):
            for dest_core in range(2):
                for part in range(2):
                    stage1(u, d, dest_core, part).wait_send()
                stage2(u, d, dest_core).wait_send()
                b1(u, d, dest_core).wait_send()
                b2(u, d, dest_core, 1 - d).wait_send()
                if u == 0:
                    b2(u, d, dest_core, d).wait_send()
        sibling_kv(u).wait_send()
        sibling_sum(u).wait_send()
        for c in q_exchange(u):
            c.wait_send()
        out_local(u).wait()
        out_remote(u).wait_send()
        out_arrival(u).wait_recv()
    for_peers(lambda r: gb(r).wait_send())
    for_peers(lambda r: ga(r).wait_send())
    for_peers(lambda r: ga_arrival(r).wait_recv())
    gain_sum = jnp.sum(ga_in[...], 0)
    gains_out[0:1] = gain_sum / q_gain[...]
    gains_out[1:2] = gain_sum / k_gain_row
    fin_g = pltpu.make_async_copy(gains_out, gains_hbm, fin_sem.at[2])
    fin_g.start()
    late_finish(1, 1)
    fin_v = pltpu.make_async_copy(dv_buf, dv_hbm.at[0], fin_sem.at[1])
    fin_v.start()
    late_finish(1, 0)
    fin_k = pltpu.make_async_copy(dk_buf, dk_hbm.at[0], fin_sem.at[0])
    fin_k.start()
    for d in range(2):
        for dest_core in range(2):
            b2(1, d, dest_core, d).wait_send()
    fin_g.wait()
    fin_k.wait()
    fin_v.wait()


def settle(dq, dk, dv, gains, dq_out, dk_out, dv_out, q_gain_out, k_gain_out, sems):
    pairs = []
    for i in range(4):
        rows = pl.ds(i * 32, 32)
        pairs.append((dq.at[0, rows], dq_out.at[0, rows]))
    pairs += [(dk, dk_out), (dv, dv_out), (gains.at[0], q_gain_out), (gains.at[1], k_gain_out)]
    copies = [pltpu.make_async_copy(a, b, sems.at[i]) for i, (a, b) in enumerate(pairs)]
    for c in copies:
        c.start()
    for c in copies:
        c.wait()


def on_device(queries, keys, values, q_gain, k_gain, out_grad, block_order):
    hbm = pl.BlockSpec(memory_space=pl.ANY)
    dma = pltpu.SemaphoreType.DMA
    sends = [dma((2, 2)), dma((2, 2, 2, 2)), dma((2, 2, 2)), dma((2,)), dma((2, 2, 2)), dma((2, 2, 2, 2)), dma((2,))]
    operands = (block_order, queries, keys, values, q_gain.reshape(1, HD), k_gain.reshape(1, HD), out_grad)
    results = pl.pallas_call(
        kernel,
        out_shape=(
            jax.ShapeDtypeStruct(queries.shape, BF),
            jax.ShapeDtypeStruct(keys.shape, BF),
            jax.ShapeDtypeStruct(values.shape, BF),
            jax.ShapeDtypeStruct((2, HD), F32),
        ),
        in_specs=[pl.BlockSpec(memory_space=pltpu.HBM)] * 7,
        out_specs=(hbm,) * 4,
        scratch_shapes=[
            pltpu.SMEM((1, 8), jnp.int32),
            pltpu.VMEM((1, HD), F32),
            pltpu.VMEM((1, HD), F32),
            pltpu.VMEM((2, HD), F32),
            pltpu.VMEM((T, HK * HD), BF),
            pltpu.VMEM((T, HK * HD), BF),
            pltpu.VMEM((2, 2, T, 1024), BF),
            pltpu.VMEM((2, 2, T, 1024), BF),
            pltpu.VMEM((2, HD, ROWS), BF),
            pltpu.VMEM((2, HD, ROWS), BF),
            pltpu.VMEM((2, HD, ROWS), F32),
            pltpu.VMEM((2, 8, ROWS), F32),
            pltpu.VMEM((HD, 256), F32),
            pltpu.VMEM((HK, 2, T, HD), BF),
            pltpu.VMEM((2, 2, 8, T, HD), BF),
            pltpu.VMEM((2, HD, KEYS), BF),
            pltpu.VMEM((2, 8, T, T), F32),
            pltpu.VMEM((2, KEYS, ROWS), BF),
            pltpu.VMEM((2, KEYS, ROWS), BF),
            pltpu.VMEM((2, 8, ROWS), F32),
            pltpu.VMEM((2, 2, 8, ROWS), F32),
            pltpu.VMEM((2, 3 * HD, ROWS), BF),
            pltpu.VMEM((2, 2, 2, T, HD), F32),
            pltpu.VMEM((2, 2, 2, T, HD), F32),
            pltpu.VMEM((2, 2, T, 1024), BF),
            pltpu.VMEM((8, HD), F32),
            pltpu.VMEM((2, 2, 2, T, HD), BF),
            pltpu.VMEM((2, 2, 2, T, HD), BF),
            pltpu.VMEM((2, 2, 2, 2, T, HD), BF),
            pltpu.VMEM((2, 2, 2, 2, T, HD), BF),
            pltpu.VMEM((2, 2, T, HD), BF),
            pltpu.VMEM((2, 2, T, HD), BF),
            pltpu.VMEM((2, 2, T, HD), F32),
            pltpu.VMEM((2, T, HD), F32),
            pltpu.VMEM((2, T, HD), F32),
            pltpu.VMEM((T, HK * HD), BF),
            pltpu.VMEM((T, HK * HD), BF),
            pltpu.VMEM((16, 1, HD), F32),
            pltpu.VMEM((16, 1, HD), F32),
            dma((9,)),
        ]
        + [s for s in sends for _ in range(2)]
        + [dma((2,)), dma((2,)), dma((2,))]
        + [dma((16,)) for _ in range(4)]
        + [dma((3,))],
        compiler_params=pltpu.CompilerParams(
            collective_id=0, has_side_effects=True, vmem_limit_bytes=44 * 1024 * 1024
        ),
    )(*(pltpu.with_memory_space_constraint(x, pltpu.HBM) for x in operands))
    return pl.pallas_call(
        settle,
        out_shape=(
            jax.ShapeDtypeStruct(queries.shape, BF),
            jax.ShapeDtypeStruct(keys.shape, BF),
            jax.ShapeDtypeStruct(values.shape, BF),
            jax.ShapeDtypeStruct((HD,), F32),
            jax.ShapeDtypeStruct((HD,), F32),
        ),
        in_specs=[hbm] * 4,
        out_specs=(hbm,) * 5,
        scratch_shapes=[dma((8,))],
        compiler_params=pltpu.CompilerParams(vmem_limit_bytes=16 * 1024 * 1024),
    )(*results)


def solution(mesh):
    placed = (
        P("dp", "ctx", None),
        P("dp", "ctx", None),
        P("dp", "ctx", None),
        P(),
        P(),
        P("dp", "ctx", None),
        P("dp", None),
    )
    return jax.shard_map(
        on_device,
        mesh=mesh,
        in_specs=placed,
        out_specs=(P("dp", "ctx", None), P("dp", "ctx", None), P("dp", "ctx", None), P(), P()),
        check_vma=False,
    )
```
